32 devices in a mesh: dp: 2 (over y), fsdp: 16 (over z, x, core).
Axes of the slice: x: 2, y: 2, z: 4, core: 2. Of those that a mesh axis runs over, the one named last changes fastest.
Arguments:
- clips_in: bfloat16 [32, 2048, 1024], P(('dp', 'fsdp')), may hold values from -6 to 6
- crop_edges: int32 [32], P(('dp', 'fsdp')), may hold values from 10 to 16, as said below
- cotangent: bfloat16 [32, 2048, 1024], P(('dp', 'fsdp')), may hold values from -6 to 6
- bottle_weights: float32 [1638400], P(('dp', 'fsdp'))
- bottle_momentum: float32 [1638400], P(('dp', 'fsdp')), may hold values from -120 to 120
- local_weights: float32 [2097152], P(('dp', 'fsdp'))
- local_momentum: float32 [2097152], P(('dp', 'fsdp')), may hold values from -6 to 6
- norm_params: float32 [5120], replicated
- norm_momentum: float32 [5120], replicated, may hold values from -6 to 6
Outputs:
- clips_out: bfloat16 [32, 2048, 1024], P(('dp', 'fsdp'))
- clips_grad: bfloat16 [32, 2048, 1024], P(('dp', 'fsdp'))
- bottle_updated: float32 [1638400], P(('dp', 'fsdp'))
- bottle_velocity: float32 [1638400], P(('dp', 'fsdp'))
- local_updated: float32 [2097152], P(('dp', 'fsdp'))
- local_velocity: float32 [2097152], P(('dp', 'fsdp'))
- norm_updated: float32 [5120], replicated
- norm_velocity: float32 [5120], replicated
The draws below stay inside these ranges and needn't reach their ends.
Inputs may be any that keep to these rules, and one draw needn't show every extreme that they name: Each clip's crop covers the top-left crop_edges x crop_edges cells of every frame; the value is one of three even sizes, and in every draw some clip has 16 and some clip the smallest.
All inputs are finite; a program needn't handle non-finite values.
Results may differ from the reference program's by a relative error of at most 0.035.
The reference program's roundings to bfloat16 on the way count: a program that leaves them out, or rounds other values in their place, can miss the bound.
Values may be sent and summed in bfloat16 or wider, within the bound.
No kernel may reach another device: no remote copies, remote signals or barrier semaphores. Data moves between devices by JAX's collectives and lax.ppermute only.
A program may use at most 192 MiB of HBM per device.

```python
import jax
import jax.numpy as jnp
from jax import lax

C = 1024
MID = 256
INNER = 512
FRAMES = 8
GRID = 16
CLIPS = 32
POSITIONS = 2048
KEYS = 512
NB = 1638400
NLW = 2097152
NP = 5120


def spread_values(key, count, deviation):
    return jax.random.normal(key, (count,), jnp.float32) * deviation


def draw_crop_edges(key, part):
    classes = jax.random.randint(key, (CLIPS,), 0, 3)
    chosen = jax.random.permutation(jax.random.fold_in(key, 7), CLIPS)
    classes = classes.at[chosen[0]].set(2)
    classes = classes.at[chosen[1]].set(0)
    smallest = 2 * (GRID * 5 // 8 // 2)
    middle_edge = 2 * (GRID * 7 // 8 // 2)
    return jnp.where(classes == 0, smallest, jnp.where(classes == 1, middle_edge, GRID)).astype(jnp.int32)


def draw_bottle_weights(key, part):
    first = spread_values(jax.random.fold_in(key, 1), 3 * C * MID, (3 * C) ** (-0.5))
    second = spread_values(jax.random.fold_in(key, 2), 9 * MID * MID, (9 * MID) ** (-0.5))
    third = spread_values(jax.random.fold_in(key, 3), MID * C, MID ** (-0.5))
    return jnp.concatenate([first, second, third])


def draw_local_weights(key, part):
    theta_part = spread_values(jax.random.fold_in(key, 1), C * INNER, 2.0 * C ** (-0.5))
    phi_part = spread_values(jax.random.fold_in(key, 2), C * INNER, 2.0 * C ** (-0.5))
    value_part = spread_values(jax.random.fold_in(key, 3), C * INNER, C ** (-0.5))
    out_part = spread_values(jax.random.fold_in(key, 4), INNER * C, INNER ** (-0.5))
    return jnp.concatenate([theta_part, phi_part, value_part, out_part])


def draw_norm_params(key, part):

    def segment(number, count, center, deviation):
        return center + spread_values(jax.random.fold_in(key, number), count, deviation)
    return jnp.concatenate([segment(1, MID, 1.0, 0.2), segment(2, MID, 0.0, 0.3), segment(3, MID, 1.0, 0.2), segment(4, MID, 0.0, 0.3), segment(5, C, 1.0, 0.2), segment(6, C, 0.0, 0.3), segment(7, C, 0.0, 1.0), segment(8, C, 0.0, 0.3)])


def shard_levels(key, dims, shards, least, high):
    level, own = 1.0, jax.random.fold_in(key, 6)
    for position, blocks in shards:
        steps = jnp.exp(jax.random.uniform(jax.random.fold_in(own, position), (blocks,), jnp.float32, least / len(shards), high / len(shards)))
        level = level * jnp.repeat(steps, dims[position] // blocks).reshape([-1 if axis == position else 1 for axis in range(len(dims))])
    return level


def gaussian(key, extent, spread, limit, cuts=(), held_as=jnp.bfloat16):
    factor_of = shard_levels(key, extent, cuts, -0.22, 0.18) if cuts else 1.0
    values = jax.random.normal(key, extent, jnp.float32) * spread * factor_of
    return jnp.minimum(jnp.maximum(values, -limit), limit).astype(held_as)


def setup_inputs(seed: int = 0) -> dict:
    key_of = jax.random.split(jax.random.key(seed), 10)
    clips_in = gaussian(key_of[0], (CLIPS, POSITIONS, C), 1.0, 6.0, ((0, 32),))
    crop_edges = draw_crop_edges(jax.random.fold_in(key_of[9], 71), 0)
    cotangent = gaussian(key_of[2], (CLIPS, POSITIONS, C), 1.0, 6.0, ((0, 32),))
    bottle_weights = draw_bottle_weights(jax.random.fold_in(key_of[9], 71), 0)
    bottle_momentum = gaussian(key_of[4], (NB,), 20.0, 120.0, ((0, 32),), jnp.float32)
    local_weights = draw_local_weights(jax.random.fold_in(key_of[9], 71), 0)
    local_momentum = gaussian(key_of[6], (NLW,), 1.0, 6.0, ((0, 32),), jnp.float32)
    norm_params = draw_norm_params(jax.random.fold_in(key_of[9], 71), 0)
    norm_momentum = gaussian(key_of[8], (NP,), 1.0, 6.0, (), jnp.float32)
    return {"clips_in": clips_in, "crop_edges": crop_edges, "cotangent": cotangent, "bottle_weights": bottle_weights, "bottle_momentum": bottle_momentum, "local_weights": local_weights, "local_momentum": local_momentum, "norm_params": norm_params, "norm_momentum": norm_momentum}


epsilon = 1e-05
learning_rate = 0.01
momentum_rate = 0.9
decay_rate = 0.0001
masked_score = -1e+30

@jax.custom_vjp
def low(v):
    return lax.optimization_barrier(v.astype(jnp.bfloat16)).astype(jnp.float32)

@jax.custom_vjp
def low_back(v):
    return v

def low_keep(v):
    return (low(v), None)

def low_pass(kept, grad):
    return (grad,)

def back_keep(v):
    return (v, None)

def back_low(kept, grad):
    return (low(grad),)
low.defvjp(low_keep, low_pass)
low_back.defvjp(back_keep, back_low)

def gelu_tanh(values):
    return jax.nn.gelu(values, approximate=True)

def product(left, right):
    return jnp.dot(left, right, precision=lax.Precision.HIGHEST, preferred_element_type=jnp.float32)

def product_cols(left, right):
    return lax.dot_general(left, right, (((1,), (1,)), ((), ())), precision=lax.Precision.HIGHEST, preferred_element_type=jnp.float32)

def edge_masks(crop_edges, frame_count, grid_edge):
    clip_count = crop_edges.shape[0]
    cells = jnp.arange(grid_edge, dtype=jnp.int32)
    edges = crop_edges[:, None, None]
    inside = (cells[None, :, None] < edges) & (cells[None, None, :] < edges)
    inside = jnp.broadcast_to(inside[:, None], (clip_count, frame_count, grid_edge, grid_edge))
    halves = jnp.arange(grid_edge // 2, dtype=jnp.int32)
    half_edges = (crop_edges // 2)[:, None, None]
    keyed = (halves[None, :, None] < half_edges) & (halves[None, None, :] < half_edges)
    keyed = jnp.broadcast_to(keyed[:, None], (clip_count, frame_count, grid_edge // 2, grid_edge // 2))
    inside = inside.reshape(clip_count, frame_count * grid_edge * grid_edge, 1).astype(jnp.float32)
    return (inside, keyed.reshape(clip_count, frame_count * (grid_edge // 2) * (grid_edge // 2)))

def split_bottle(flat, channels, middle):
    first = 3 * channels * middle
    second = first + 9 * middle * middle
    return (flat[:first].reshape(3, channels, middle), flat[first:second].reshape(9, middle, middle), flat[second:].reshape(middle, channels))

def split_local(flat, channels, inner_width):
    block = channels * inner_width
    return (flat[:block].reshape(channels, inner_width), flat[block:2 * block].reshape(channels, inner_width), flat[2 * block:3 * block].reshape(channels, inner_width), flat[3 * block:].reshape(inner_width, channels))

def split_norms(vector, channels, middle):
    sizes_list = [middle, middle, middle, middle, channels, channels, channels, channels]
    pieces_out = []
    offset = 0
    for length in sizes_list:
        pieces_out.append(vector[offset:offset + length])
        offset = offset + length
    return pieces_out

def shift_frames(values, offset):
    padded = jnp.pad(values, ((1, 1), (0, 0), (0, 0), (0, 0)))
    return padded[1 + offset:1 + offset + FRAMES]

def shift_cells(values, row_step, col_step):
    padded = jnp.pad(values, ((0, 0), (1, 1), (1, 1), (0, 0)))
    return padded[:, 1 + row_step:1 + row_step + GRID, 1 + col_step:1 + col_step + GRID]

def forward(clips, bottle, local, norms, inside, keyed):
    bottle = low(bottle)
    local = low(local)
    weight_a, weight_b, weight_c = split_bottle(bottle, C, MID)
    w_theta, w_phi, w_value, w_out = split_local(local, C, INNER)
    gain_a, shift_a, gain_b, shift_b, gain_c, shift_c, gain_n, shift_n = split_norms(norms, C, MID)
    cell_total = jnp.sum(inside)

    def batch_norm(values, gain, shift):
        mean = lax.optimization_barrier(jnp.sum(values * inside, axis=(0, 1))) / cell_total
        square = lax.optimization_barrier(jnp.sum(values * values * inside, axis=(0, 1))) / cell_total
        return (values - mean) * lax.rsqrt(square - mean * mean + epsilon) * gain + shift
    input_cells = clips * inside

    def conv_frames(clip_one):
        grid_values = clip_one.reshape(FRAMES, GRID, GRID, C)
        total = jnp.zeros((POSITIONS, MID), jnp.float32)
        for offset in range(3):
            total = total + product(shift_frames(grid_values, offset - 1).reshape(POSITIONS, C), weight_a[offset])
        return total

    def conv_cells(clip_one):
        grid_values = clip_one.reshape(FRAMES, GRID, GRID, MID)
        total = jnp.zeros((POSITIONS, MID), jnp.float32)
        for row_step in (-1, 0, 1):
            for col_step in (-1, 0, 1):
                tap = 3 * (row_step + 1) + col_step + 1
                total = total + product(shift_cells(grid_values, row_step, col_step).reshape(POSITIONS, MID), weight_b[tap])
        return total

    def conv_expand(clip_one):
        return product(clip_one, weight_c)
    pre_a = low_back(lax.map(jax.checkpoint(conv_frames), input_cells))
    hidden_a = low(gelu_tanh(batch_norm(pre_a, gain_a, shift_a)) * inside)
    pre_b = low_back(lax.map(jax.checkpoint(conv_cells), hidden_a))
    hidden_b = low(gelu_tanh(batch_norm(pre_b, gain_b, shift_b)) * inside)
    pre_c = low_back(lax.map(jax.checkpoint(conv_expand), hidden_b))
    mixed = low(gelu_tanh(batch_norm(pre_c, gain_c, shift_c) + input_cells) * inside)
    clip_count = clips.shape[0]
    pooled = low(lax.optimization_barrier(jnp.mean(mixed.reshape(clip_count, FRAMES, GRID // 2, 2, GRID // 2, 2, C), axis=(3, 5))).reshape(clip_count, KEYS, C))

    def attend(pieces):
        mixed_one, pooled_one, keyed_one = pieces
        query = low(low_back(product(mixed_one, w_theta)))
        key_rows = low(low_back(product(pooled_one, w_phi)))
        value_rows = low(low_back(product(pooled_one, w_value)))
        scores = low_back(product_cols(query, key_rows)) * INNER ** (-0.5)
        scores = jnp.where(keyed_one[None, :], scores, masked_score)
        probs = jax.nn.softmax(scores, axis=-1)
        attended = low(low_back(product(low(probs), value_rows)))
        return product(attended, w_out)
    pre_w = low_back(lax.map(jax.checkpoint(attend), (mixed, pooled, keyed)))
    return (batch_norm(pre_w, gain_n, shift_n) + mixed) * inside

def reference(clips_in, crop_edges, cotangent, bottle_weights, bottle_momentum, local_weights, local_momentum, norm_params, norm_momentum):
    inside, keyed = edge_masks(crop_edges, FRAMES, GRID)

    def wrapped(clips, bottle, local, norms):
        return forward(clips, bottle, local, norms, inside, keyed)
    clips_out, pullback = jax.vjp(wrapped, clips_in.astype(jnp.float32), bottle_weights, local_weights, norm_params)
    clips_grad, bottle_grad, local_grad, norm_grad = pullback(cotangent.astype(jnp.float32))
    bottle_velocity = momentum_rate * bottle_momentum + bottle_grad / CLIPS + decay_rate * bottle_weights
    local_velocity = momentum_rate * local_momentum + local_grad / CLIPS + decay_rate * local_weights
    norm_velocity = momentum_rate * norm_momentum + norm_grad / CLIPS
    bottle_updated = bottle_weights - learning_rate * bottle_velocity
    local_updated = local_weights - learning_rate * local_velocity
    norm_updated = norm_params - learning_rate * norm_velocity
    return (clips_out.astype(jnp.bfloat16), clips_grad.astype(jnp.bfloat16), bottle_updated, bottle_velocity, local_updated, local_velocity, norm_updated, norm_velocity)
```

```python
import jax
import jax.numpy as jnp
from jax import lax
from jax.sharding import PartitionSpec as P

MID = 256
INNER = 512
FRAMES = 8
GRID = 16


epsilon = 1e-05
learning_rate = 0.01
momentum_rate = 0.9
decay_rate = 0.0001
masked_score = -1e30


def gelu_tanh(values):
    return jax.nn.gelu(values, approximate=True)


def gelu_back(values, upstream):
    result, pullback = jax.vjp(gelu_tanh, values)
    return pullback(upstream)[0]


def product(left, right):
    return jnp.dot(left, right, preferred_element_type=jnp.float32)


def product_rows(left, right):
    return lax.dot_general(
        left, right, (((0,), (0,)), ((), ())), preferred_element_type=jnp.float32
    )


def product_cols(left, right):
    return lax.dot_general(
        left, right, (((1,), (1,)), ((), ())), preferred_element_type=jnp.float32
    )


def shift_frames(values, offset):
    frame_count = values.shape[1]
    padded = jnp.pad(values, ((0, 0), (1, 1), (0, 0), (0, 0), (0, 0)))
    return padded[:, 1 + offset : 1 + offset + frame_count]


def shift_cells(values, row_step, col_step):
    grid_edge = values.shape[2]
    padded = jnp.pad(values, ((0, 0), (0, 0), (1, 1), (1, 1), (0, 0)))
    return padded[
        :, :, 1 + row_step : 1 + row_step + grid_edge, 1 + col_step : 1 + col_step + grid_edge
    ]


def edge_masks(crop_edges, frame_count, grid_edge):
    clip_count = crop_edges.shape[0]
    cells = jnp.arange(grid_edge, dtype=jnp.int32)
    edges = crop_edges[:, None, None]
    inside = (cells[None, :, None] < edges) & (cells[None, None, :] < edges)
    inside = jnp.broadcast_to(inside[:, None], (clip_count, frame_count, grid_edge, grid_edge))
    halves = jnp.arange(grid_edge // 2, dtype=jnp.int32)
    half_edges = (crop_edges // 2)[:, None, None]
    keyed = (halves[None, :, None] < half_edges) & (halves[None, None, :] < half_edges)
    keyed = jnp.broadcast_to(
        keyed[:, None], (clip_count, frame_count, grid_edge // 2, grid_edge // 2)
    )
    inside = inside.reshape(clip_count, frame_count * grid_edge * grid_edge, 1).astype(jnp.float32)
    return (inside, keyed.reshape(clip_count, frame_count * (grid_edge // 2) * (grid_edge // 2)))


def split_norms(vector, channels, middle):
    sizes_list = [middle, middle, middle, middle, channels, channels, channels, channels]
    pieces_out = []
    offset = 0
    for length in sizes_list:
        pieces_out.append(vector[offset : offset + length])
        offset = offset + length
    return pieces_out


AXES = ("dp", "fsdp")


def device_count():
    return lax.axis_size("dp") * lax.axis_size("fsdp")


def device_bit(bit):
    return (lax.axis_index(AXES) >> bit) & 1


def bit_count():
    count = device_count()
    bits = count.bit_length() - 1
    assert count == 1 << bits
    return bits


def swap(values, mask):
    count = device_count()
    return lax.ppermute(values, AXES, [(i, i ^ mask) for i in range(count)])


def sum_devices(values):
    bits = bit_count()
    groups = [[0]]
    low, high = 1, bits - 1
    while low <= high:
        groups.append([low, high] if low < high else [low])
        low, high = low + 1, high - 1
    for group in groups:
        if len(group) == 1:
            values = values + swap(values, 1 << group[0])
        else:
            one, two = 1 << group[0], 1 << group[1]
            near, far, both = swap(values, one), swap(values, two), swap(values, one | two)
            values = (values + near) + (far + both)
    return values


def travel_order():
    bits = bit_count()
    order = list(range(bits - 2, 1, -1)) + [bits - 1, 1, 0]
    return [bit for bit in dict.fromkeys(order) if 0 <= bit < bits]


def gather_rows(rows):
    present = []
    values = rows
    for bit in travel_order():
        other = swap(values, 1 << bit)
        mine = device_bit(bit) == 1
        position = sum(1 for have in present if have > bit)
        values = jnp.stack(
            [jnp.where(mine, other, values), jnp.where(mine, values, other)], axis=position
        )
        present.append(bit)
    return values.reshape((-1,) + rows.shape[1:])


def scatter_rows(values):
    bits = bit_count()
    width = values.shape[1]
    values = values.reshape((2,) * bits + (-1, width))
    present = list(range(bits - 1, -1, -1))
    for bit in reversed(travel_order()):
        position = present.index(bit)
        low = lax.index_in_dim(values, 0, position, keepdims=False)
        high = lax.index_in_dim(values, 1, position, keepdims=False)
        mine = device_bit(bit) == 1
        keep, send = jnp.where(mine, high, low), jnp.where(mine, low, high)
        got = swap(send, 1 << bit)
        values = keep.astype(jnp.float32) + got.astype(jnp.float32)
        present.remove(bit)
        if present:
            values = values.astype(jnp.bfloat16)
    return values


def batch_norm(values, inside, local_cells, gain, shift):
    width = values.shape[1]
    sums = sum_devices(
        jnp.concatenate(
            [
                jnp.sum(values * inside, axis=0)[None],
                jnp.sum(values * values * inside, axis=0)[None],
                jnp.full((1, width), local_cells),
            ]
        )
    )
    first, second, cell_total = sums[0], sums[1], sums[2, 0]
    mean = first / cell_total
    scale = lax.rsqrt(second / cell_total - mean * mean + epsilon)
    normed = (values - mean) * scale
    return (normed * gain + shift, normed, scale, cell_total)


def batch_norm_back(upstream, normed, scale, cell_total, inside, gain):
    sums = sum_devices(
        jnp.stack([jnp.sum(upstream * inside, axis=0), jnp.sum(upstream * normed * inside, axis=0)])
    )
    shift_grad, gain_grad = sums[0], sums[1]
    back = inside * gain * scale * (upstream - (shift_grad + normed * gain_grad) / cell_total)
    return (back, gain_grad, shift_grad)


def on_device(
    clips_in,
    crop_edges,
    cotangent,
    bottle_weights,
    bottle_momentum,
    local_weights,
    local_momentum,
    norm_params,
    norm_momentum,
):
    clip_count, position_count, channels = clips_in.shape
    middle = MID
    inner_width = INNER
    frame_count = FRAMES
    grid_edge = GRID
    half_edge = grid_edge // 2
    key_count = frame_count * half_edge * half_edge
    row_count = clip_count * position_count
    shaped = (clip_count, frame_count, grid_edge, grid_edge)
    inside, keyed = edge_masks(crop_edges, frame_count, grid_edge)
    inside = inside.reshape(row_count, 1)
    local_cells = jnp.sum(inside)
    gain_a, shift_a, gain_b, shift_b, gain_c, shift_c, gain_n, shift_n = split_norms(
        norm_params, channels, middle
    )
    score_scale = inner_width ** (-0.5)
    bottle_full = gather_rows(bottle_weights.astype(jnp.bfloat16).reshape(-1, middle))
    weight_a = bottle_full[: 3 * channels].reshape(3, channels, middle)
    weight_b = bottle_full[3 * channels : 3 * channels + 9 * middle].reshape(9, middle, middle)
    weight_c = bottle_full[3 * channels + 9 * middle :].reshape(middle, channels)
    local_full = lax.all_gather(
        local_weights.astype(jnp.bfloat16).reshape(-1, inner_width), AXES, axis=0, tiled=True
    )
    input_cells = clips_in.reshape(row_count, channels) * inside.astype(jnp.bfloat16)
    input_grid = input_cells.reshape(shaped + (channels,))
    pre_a = jnp.zeros((row_count, middle), jnp.float32)
    for offset in range(3):
        pre_a = pre_a + product(
            shift_frames(input_grid, offset - 1).reshape(row_count, channels), weight_a[offset]
        )
    norm_a, normed_a, scale_a, cell_total = batch_norm(pre_a, inside, local_cells, gain_a, shift_a)
    hidden_a = (gelu_tanh(norm_a) * inside).astype(jnp.bfloat16)
    hidden_grid = hidden_a.reshape(shaped + (middle,))
    pre_b = jnp.zeros((row_count, middle), jnp.float32)
    for row_step in (-1, 0, 1):
        for col_step in (-1, 0, 1):
            tap = 3 * (row_step + 1) + col_step + 1
            pre_b = pre_b + product(
                shift_cells(hidden_grid, row_step, col_step).reshape(row_count, middle),
                weight_b[tap],
            )
    norm_b, normed_b, scale_b, cell_total = batch_norm(pre_b, inside, local_cells, gain_b, shift_b)
    hidden_b = (gelu_tanh(norm_b) * inside).astype(jnp.bfloat16)
    pre_c = product(hidden_b, weight_c)
    norm_c, normed_c, scale_c, cell_total = batch_norm(pre_c, inside, local_cells, gain_c, shift_c)
    joined = norm_c + input_cells.astype(jnp.float32)
    mixed = (gelu_tanh(joined) * inside).astype(jnp.bfloat16)
    w_theta, w_phi, w_value = (
        local_full[:channels],
        local_full[channels : 2 * channels],
        local_full[2 * channels : 3 * channels],
    )
    w_out = local_full[3 * channels :].reshape(inner_width, channels)
    pooled = (
        jnp.mean(
            mixed.astype(jnp.float32).reshape(
                clip_count, frame_count, half_edge, 2, half_edge, 2, channels
            ),
            axis=(3, 5),
        )
        .astype(jnp.bfloat16)
        .reshape(clip_count * key_count, channels)
    )
    query = product(mixed, w_theta).astype(jnp.bfloat16)
    key_rows = product(pooled, w_phi).astype(jnp.bfloat16)
    value_rows = product(pooled, w_value).astype(jnp.bfloat16)
    query_clips = query.reshape(clip_count, position_count, inner_width)
    key_clips = key_rows.reshape(clip_count, key_count, inner_width)
    value_clips = value_rows.reshape(clip_count, key_count, inner_width)

    def attend(pieces):
        query_one, key_one, value_one, keyed_one = pieces
        scores = jnp.where(
            keyed_one[None, :], product_cols(query_one, key_one) * score_scale, masked_score
        )
        peak = jnp.max(scores, axis=1, keepdims=True)
        weights = jnp.exp(scores - peak)
        weight_sum = jnp.sum(weights, axis=1, keepdims=True)
        attended_one = product((weights / weight_sum).astype(jnp.bfloat16), value_one).astype(
            jnp.bfloat16
        )
        return (attended_one, peak + jnp.log(weight_sum))

    attended, log_sums = lax.map(attend, (query_clips, key_clips, value_clips, keyed))
    attended_rows = attended.reshape(row_count, inner_width)
    pre_w = product(attended_rows, w_out)
    norm_w, normed_w, scale_w, cell_total = batch_norm(pre_w, inside, local_cells, gain_n, shift_n)
    clips_out = (
        ((norm_w + mixed.astype(jnp.float32)) * inside)
        .astype(jnp.bfloat16)
        .reshape(clip_count, position_count, channels)
    )
    grad_out = cotangent.reshape(row_count, channels).astype(jnp.float32) * inside
    back_w, gain_n_grad, shift_n_grad = batch_norm_back(
        grad_out, normed_w, scale_w, cell_total, inside, gain_n
    )
    back_w = back_w.astype(jnp.bfloat16)
    grad_w_out = product_rows(attended_rows, back_w)
    grad_attended = product_cols(back_w, w_out).astype(jnp.bfloat16)
    grad_clips = grad_attended.reshape(clip_count, position_count, inner_width)

    def attend_back(pieces):
        query_one, key_one, value_one, keyed_one, lse_one, grad_one = pieces
        scores = jnp.where(
            keyed_one[None, :], product_cols(query_one, key_one) * score_scale, masked_score
        )
        probs = jnp.exp(scores - lse_one)
        grad_probs = product_cols(grad_one, value_one)
        grad_scores = probs * (grad_probs - jnp.sum(probs * grad_probs, axis=1, keepdims=True))
        grad_dots = (grad_scores * score_scale).astype(jnp.bfloat16)
        grad_query_one = product(grad_dots, key_one).astype(jnp.bfloat16)
        grad_key_one = product_rows(grad_dots, query_one).astype(jnp.bfloat16)
        grad_value_one = product_rows(probs.astype(jnp.bfloat16), grad_one).astype(jnp.bfloat16)
        return (grad_query_one, grad_key_one, grad_value_one)

    grad_query, grad_key, grad_value = lax.map(
        attend_back, (query_clips, key_clips, value_clips, keyed, log_sums, grad_clips)
    )
    grad_query = grad_query.reshape(row_count, inner_width)
    grad_key = grad_key.reshape(clip_count * key_count, inner_width)
    grad_value = grad_value.reshape(clip_count * key_count, inner_width)
    grad_theta = product_rows(mixed, grad_query)
    grad_phi = product_rows(pooled, grad_key)
    grad_gather = product_rows(pooled, grad_value)
    grad_pooled = product_cols(grad_key, w_phi) + product_cols(grad_value, w_value)
    spread = jnp.broadcast_to(
        grad_pooled.reshape(clip_count, frame_count, half_edge, 1, half_edge, 1, channels) * 0.25,
        (clip_count, frame_count, half_edge, 2, half_edge, 2, channels),
    ).reshape(row_count, channels)
    grad_mixed = grad_out + product_cols(grad_query, w_theta) + spread
    low = jnp.bfloat16
    local_shard = scatter_rows(
        jnp.concatenate(
            [
                grad_theta.astype(low),
                grad_phi.astype(low),
                grad_gather.astype(low),
                grad_w_out.astype(low).reshape(2 * inner_width, inner_width),
            ]
        )
    ).reshape(-1)
    grad_joined = gelu_back(joined, grad_mixed * inside)
    back_c, gain_c_grad, shift_c_grad = batch_norm_back(
        grad_joined, normed_c, scale_c, cell_total, inside, gain_c
    )
    back_c = back_c.astype(jnp.bfloat16)
    grad_weight_c = product_rows(hidden_b, back_c)
    grad_hidden_b = product_cols(back_c, weight_c)
    back_b, gain_b_grad, shift_b_grad = batch_norm_back(
        gelu_back(norm_b, grad_hidden_b * inside), normed_b, scale_b, cell_total, inside, gain_b
    )
    back_b = back_b.astype(jnp.bfloat16)
    grad_taps = []
    grad_hidden_a = jnp.zeros(shaped + (middle,), jnp.float32)
    for row_step in (-1, 0, 1):
        for col_step in (-1, 0, 1):
            tap = 3 * (row_step + 1) + col_step + 1
            grad_taps.append(
                product_rows(
                    shift_cells(hidden_grid, row_step, col_step).reshape(row_count, middle), back_b
                )
            )
            reach = product_cols(back_b, weight_b[tap]).reshape(shaped + (middle,))
            grad_hidden_a = grad_hidden_a + shift_cells(reach, -row_step, -col_step)
    grad_weight_b = jnp.stack(grad_taps)
    grad_hidden_a = grad_hidden_a.reshape(row_count, middle)
    back_a, gain_a_grad, shift_a_grad = batch_norm_back(
        gelu_back(norm_a, grad_hidden_a * inside), normed_a, scale_a, cell_total, inside, gain_a
    )
    back_a = back_a.astype(jnp.bfloat16)
    grad_frames = []
    grad_input = jnp.zeros(shaped + (channels,), jnp.float32)
    for offset in range(3):
        grad_frames.append(
            product_rows(shift_frames(input_grid, offset - 1).reshape(row_count, channels), back_a)
        )
        reach = product_cols(back_a, weight_a[offset]).reshape(shaped + (channels,))
        grad_input = grad_input + shift_frames(reach, 1 - offset)
    grad_weight_a = jnp.stack(grad_frames)
    clips_grad = ((grad_input.reshape(row_count, channels) + grad_joined) * inside).astype(
        jnp.bfloat16
    )
    clips_grad = clips_grad.reshape(clip_count, position_count, channels)
    bottle_shard = scatter_rows(
        jnp.concatenate(
            [
                grad_weight_a.astype(low).reshape(-1, middle),
                grad_weight_b.astype(low).reshape(-1, middle),
                grad_weight_c.astype(low).reshape(-1, middle),
            ]
        )
    ).reshape(-1)
    clips_total = clip_count * lax.axis_size("dp") * lax.axis_size("fsdp")
    norm_grad = jnp.concatenate(
        [
            gain_a_grad,
            shift_a_grad,
            gain_b_grad,
            shift_b_grad,
            gain_c_grad,
            shift_c_grad,
            gain_n_grad,
            shift_n_grad,
        ]
    )
    bottle_velocity = (
        momentum_rate * bottle_momentum + bottle_shard / clips_total + decay_rate * bottle_weights
    )
    local_velocity = (
        momentum_rate * local_momentum + local_shard / clips_total + decay_rate * local_weights
    )
    norm_velocity = momentum_rate * norm_momentum + norm_grad / clips_total
    bottle_updated = bottle_weights - learning_rate * bottle_velocity
    local_updated = local_weights - learning_rate * local_velocity
    norm_updated = norm_params - learning_rate * norm_velocity
    return (
        clips_out,
        clips_grad,
        bottle_updated,
        bottle_velocity,
        local_updated,
        local_velocity,
        norm_updated,
        norm_velocity,
    )


def solution(mesh):
    placed = (
        P(("dp", "fsdp"), None, None),
        P(("dp", "fsdp")),
        P(("dp", "fsdp"), None, None),
        P(("dp", "fsdp")),
        P(("dp", "fsdp")),
        P(("dp", "fsdp")),
        P(("dp", "fsdp")),
        P(),
        P(),
    )
    return jax.shard_map(
        on_device,
        mesh=mesh,
        in_specs=placed,
        out_specs=(
            P(("dp", "fsdp"), None, None),
            P(("dp", "fsdp"), None, None),
            P(("dp", "fsdp")),
            P(("dp", "fsdp")),
            P(("dp", "fsdp")),
            P(("dp", "fsdp")),
            P(),
            P(),
        ),
        check_vma=False,
    )
```

```python
import jax
import jax.numpy as jnp
from jax import lax
from jax.experimental import pallas as pl
from jax.experimental.pallas import tpu as pltpu
from jax.sharding import PartitionSpec as P

MID = 256
INNER = 512
FRAMES = 8
GRID = 16
CELLS = GRID * GRID
HALF = CELLS // 4

epsilon = 1e-05
learning_rate = 0.01
momentum_rate = 0.9
decay_rate = 0.0001
masked_score = -1e30
curve = 0.7978845608028654
cubic = 0.044715

VMEM = 32 * 1024 * 1024
low = jnp.bfloat16
full = jnp.float32


AXES = ("dp", "fsdp")


def device_count():
    return lax.axis_size("dp") * lax.axis_size("fsdp")


def device_bit(bit):
    return (lax.axis_index(AXES) >> bit) & 1


def bit_count():
    count = device_count()
    bits = count.bit_length() - 1
    assert count == 1 << bits
    return bits


def swap(values, mask):
    count = device_count()
    return lax.ppermute(values, AXES, [(i, i ^ mask) for i in range(count)])


def sum_devices(values):
    bits = bit_count()
    groups = [[0]]
    low, high = 1, bits - 1
    while low <= high:
        groups.append([low, high] if low < high else [low])
        low, high = low + 1, high - 1
    for group in groups:
        if len(group) == 1:
            values = values + swap(values, 1 << group[0])
        else:
            one, two = 1 << group[0], 1 << group[1]
            near, far, both = swap(values, one), swap(values, two), swap(values, one | two)
            values = (values + near) + (far + both)
    return values


def travel_order():
    bits = bit_count()
    order = list(range(bits - 2, 1, -1)) + [bits - 1, 1, 0]
    return [bit for bit in dict.fromkeys(order) if 0 <= bit < bits]


def gather_rows(rows):
    present = []
    values = rows
    for bit in travel_order():
        other = swap(values, 1 << bit)
        mine = device_bit(bit) == 1
        position = sum(1 for have in present if have > bit)
        values = jnp.stack(
            [jnp.where(mine, other, values), jnp.where(mine, values, other)], axis=position
        )
        present.append(bit)
    return values.reshape((-1,) + rows.shape[1:])


class Scatter:
    def __init__(self, values):
        bits = bit_count()
        self.values = values.reshape((2,) * bits + (-1, values.shape[1]))
        self.present = list(range(bits - 1, -1, -1))
        self.order = list(reversed(travel_order()))
        self.got = None

    def send(self):
        if self.got is not None:
            self.values = (self.keep.astype(full) + self.got.astype(full)).astype(low)
        bit = self.order.pop(0)
        position = self.present.index(bit)
        upper = lax.index_in_dim(self.values, 1, position, keepdims=False)
        lower = lax.index_in_dim(self.values, 0, position, keepdims=False)
        mine = device_bit(bit) == 1
        self.keep = jnp.where(mine, upper, lower)
        self.got = swap(jnp.where(mine, lower, upper), 1 << bit)
        self.present.remove(bit)

    def after(self, other):
        other, self.got = lax.optimization_barrier((other, self.got))
        return other

    def finish(self):
        while self.order:
            self.send()
        return self.keep.astype(full) + self.got.astype(full)


def dot(left, right):
    return jnp.dot(left, right, preferred_element_type=full)


def dot_cols(left, right):
    return lax.dot_general(left, right, (((1,), (1,)), ((), ())), preferred_element_type=full)


def dot_rows(left, right):
    return lax.dot_general(left, right, (((0,), (0,)), ((), ())), preferred_element_type=full)


def gelu(v):
    return 0.5 * v * (1.0 + jnp.tanh(curve * (v + cubic * (v * v * v))))


def gelu_slope(v):
    square = v * v
    bend = jnp.tanh(v * (curve + (curve * cubic) * square))
    half = 0.5 * v
    return 0.5 + 0.5 * bend + half * (1.0 - bend * bend) * (curve + (3.0 * curve * cubic) * square)


def inside_of(edge, rows):
    cell = lax.broadcasted_iota(jnp.int32, (rows, 1), 0) & (CELLS - 1)
    return (((cell >> 4) < edge) & ((cell & 15) < edge)).astype(full)


def total(values):
    return jnp.sum(values, axis=0, keepdims=True)


def moments(sums_ref, count):
    mean = sums_ref[0:1] / count
    return mean, lax.rsqrt(sums_ref[1:2] / count - mean * mean + epsilon)


def norm_terms(sums_ref, params_ref, count):
    mean, root = moments(sums_ref, count)
    scale = root * params_ref[0:1]
    return scale, params_ref[1:2] - mean * scale, root, -mean * root


def back_terms(shift_grad, gain_grad, scale, root, root_offset, count):
    slope = -(scale * gain_grad * root) / count
    offset = -(scale * (shift_grad + gain_grad * root_offset)) / count
    return slope, offset


def add_to(ref, row, value):
    @pl.when(pl.program_id(0) == 0)
    def _():
        ref[row : row + 1, :] = value

    @pl.when(pl.program_id(0) != 0)
    def _():
        ref[row : row + 1, :] += value


def call(kernel, steps, ins, outs, scratch=(), flops=0, name=None, aliases=None):
    def spec(shape, rows):
        if rows == "smem":
            return pl.BlockSpec(memory_space=pltpu.SMEM)
        if isinstance(rows, pl.BlockSpec):
            return rows
        if rows is None:
            return pl.BlockSpec(shape, lambda i: (0,) * len(shape))
        return pl.BlockSpec((rows,) + tuple(shape[1:]), lambda i: (i,) + (0,) * (len(shape) - 1))

    size = sum(a.size * a.dtype.itemsize for a, _ in ins) + sum(
        a.size * a.dtype.itemsize for a, _ in outs
    )
    return pl.pallas_call(
        kernel,
        grid=(steps,),
        in_specs=[spec(a.shape, rows) for a, rows in ins],
        out_specs=[spec(a.shape, rows) for a, rows in outs],
        out_shape=[a for a, _ in outs],
        scratch_shapes=list(scratch),
        compiler_params=pltpu.CompilerParams(vmem_limit_bytes=VMEM),
        cost_estimate=pl.CostEstimate(flops=flops, bytes_accessed=size, transcendentals=0),
        input_output_aliases=aliases or {},
        name=name,
    )(*[a for a, _ in ins])


def shape(dims, dtype):
    return jax.ShapeDtypeStruct(dims, dtype)


def conv_a_kernel(edge_ref, x_ref, w_ref, pre_ref, sums_ref):
    step = pl.program_id(0)
    rows = x_ref.shape[0]
    per = rows // CELLS
    steps = FRAMES // per
    for one in range(per):
        frame = step * per + one
        values = x_ref[one * CELLS : (one + 1) * CELLS, :]

        here = pl.ds(pl.multiple_of(frame * CELLS, CELLS), CELLS)
        after = pl.ds(pl.multiple_of((frame + 1) * CELLS, CELLS), CELLS)
        before = pl.ds(pl.multiple_of(jnp.maximum(frame - 1, 0) * CELLS, CELLS), CELLS)
        middle = dot(values, w_ref[1])

        @pl.when(frame == 0)
        def _():
            pre_ref[here, :] = middle

        @pl.when(frame > 0)
        def _():
            pre_ref[here, :] += middle
            pre_ref[before, :] += dot(values, w_ref[2])

        @pl.when(frame < FRAMES - 1)
        def _():
            pre_ref[after, :] = dot(values, w_ref[0])

    @pl.when(step == steps - 1)
    def _():
        edge = edge_ref[0]
        inside = inside_of(edge, CELLS)

        def body(frame, sums):
            v = pre_ref[pl.ds(pl.multiple_of(frame * CELLS, CELLS), CELLS), :]
            m = v * inside
            return sums[0] + total(m), sums[1] + total(m * v)

        zero = jnp.zeros((1, pre_ref.shape[1]), full)
        first, second = lax.fori_loop(0, FRAMES, body, (zero, zero))
        sums_ref[0:1, :] = first
        sums_ref[1:2, :] = second
        sums_ref[2:3, :] = jnp.full(zero.shape, (FRAMES * edge * edge).astype(full))


def shift_columns(values, step):
    if step == 0:
        return values
    rows = values.shape[0]
    column = lax.broadcasted_iota(jnp.int32, (rows, 1), 0) & (GRID - 1)
    edge = GRID - 1 if step == 1 else 0
    moved = pltpu.roll(values, (-step) % rows, 0)
    return jnp.where(column == edge, 0.0, moved)


def spread_taps(values, wide_ref):
    wide_ref[:GRID, :] = jnp.zeros((GRID, 3 * MID), low)
    wide_ref[GRID + CELLS :, :] = jnp.zeros((GRID, 3 * MID), low)
    for step in (-1, 0, 1):
        wide_ref[GRID : GRID + CELLS, (step + 1) * MID : (step + 2) * MID] = shift_columns(
            values, step
        ).astype(low)


def conv_b_kernel(edge_ref, count_ref, pre_ref, sums_a_ref, params_ref, w_ref, hidden_ref, out_ref, sums_ref, wide_ref):
    count = count_ref[2:3, 0:1]
    inside = inside_of(edge_ref[0], CELLS)
    scale, offset, _, _ = norm_terms(sums_a_ref, params_ref, count)
    first = jnp.zeros((1, MID), full)
    second = first
    for one in range(pre_ref.shape[0] // CELLS):
        part = slice(one * CELLS, (one + 1) * CELLS)
        hidden = gelu(pre_ref[part, :] * scale + offset) * inside
        hidden_ref[part, :] = hidden.astype(low)
        wide = wide_ref.at[one]
        spread_taps(hidden, wide)
        values = dot(wide[0:CELLS, :], w_ref[0])
        values += dot(wide[GRID : GRID + CELLS, :], w_ref[1])
        values += dot(wide[2 * GRID : 2 * GRID + CELLS, :], w_ref[2])
        out_ref[part, :] = values
        m = values * inside
        first += total(m)
        second += total(m * values)
    add_to(sums_ref, 0, first)
    add_to(sums_ref, 1, second)


def conv_c_kernel(edge_ref, count_ref, pre_ref, sums_b_ref, params_ref, w_ref, hidden_ref, sums_ref):
    count = count_ref[2:3, 0:1]
    inside = inside_of(edge_ref[0], pre_ref.shape[0])
    scale, offset, _, _ = norm_terms(sums_b_ref, params_ref, count)
    hidden = (gelu(pre_ref[...] * scale + offset) * inside).astype(low)
    hidden_ref[...] = hidden
    values = dot(hidden, w_ref[...])
    add_to(sums_ref, 0, total(values))
    add_to(sums_ref, 1, total(values * values))


def pool_matrix(rows, columns, weight):
    pooled = lax.broadcasted_iota(jnp.int32, (rows, columns), 0) & (HALF - 1)
    cell = lax.broadcasted_iota(jnp.int32, (rows, columns), 1)
    same = ((cell >> 5) == (pooled >> 3)) & (((cell >> 1) & 7) == (pooled & 7))
    return jnp.where(same, weight, 0.0).astype(low)


def spread_matrix(rows, columns, weight):
    cell = lax.broadcasted_iota(jnp.int32, (rows, columns), 0)
    pooled = lax.broadcasted_iota(jnp.int32, (rows, columns), 1) & (HALF - 1)
    same = ((cell >> 5) == (pooled >> 3)) & (((cell >> 1) & 7) == (pooled & 7))
    return jnp.where(same, weight, 0.0).astype(low)


def embed_kernel(edge_ref, count_ref, hidden_ref, x_ref, sums_c_ref, params_ref, w_c_ref, w_ref, mixed_ref, pooled_ref, query_ref, key_ref, value_ref):
    count = count_ref[2:3, 0:1]
    inside = inside_of(edge_ref[0], CELLS)
    scale, offset, _, _ = norm_terms(sums_c_ref, params_ref, count)
    pool = pool_matrix(HALF, CELLS, 0.25)
    for one in range(hidden_ref.shape[0] // CELLS):
        part = slice(one * CELLS, (one + 1) * CELLS)
        piece = slice(one * HALF, (one + 1) * HALF)
        joined = dot(hidden_ref[part, :], w_c_ref[...]) * scale + offset + x_ref[part, :].astype(full)
        mixed = (gelu(joined) * inside).astype(low)
        mixed_ref[part, :] = mixed
        query_ref[part, :] = dot(mixed, w_ref[0]).astype(low)
        pooled = dot(pool, mixed).astype(low)
        pooled_ref[piece, :] = pooled
        key_ref[piece, :] = dot(pooled, w_ref[1]).astype(low)
        value_ref[piece, :] = dot(pooled, w_ref[2]).astype(low)


def attend_kernel(edge_ref, query_ref, key_ref, value_ref, w_out_ref, cot_ref, probs_ref, attended_ref, pre_ref, sums_ref):
    edge = edge_ref[0]
    rows = query_ref.shape[0]
    inside = inside_of(edge, rows)
    keys = key_ref.shape[0]
    spot = lax.broadcasted_iota(jnp.int32, (1, keys), 1)
    keyed = (((spot >> 3) & 7) * 2 < edge) & ((spot & 7) * 2 < edge)
    scores = dot_cols(query_ref[...], key_ref[...]) * (query_ref.shape[1] ** -0.5)
    scores = jnp.where(keyed, scores, masked_score)
    weights = jnp.exp(scores - jnp.max(scores, axis=1, keepdims=True))
    probs = weights * (inside / jnp.sum(weights, axis=1, keepdims=True))
    probs_ref[...] = probs
    attended = dot(probs.astype(low), value_ref[...]).astype(low)
    attended_ref[...] = attended
    values = dot(attended, w_out_ref[...])
    pre_ref[...] = values
    upstream = cot_ref[...].astype(full) * inside
    add_to(sums_ref, 0, total(values))
    add_to(sums_ref, 1, total(values * values))
    add_to(sums_ref, 2, total(upstream))
    add_to(sums_ref, 3, total(upstream * values))


def attend_back_kernel(edge_ref, count_ref, pre_ref, mixed_ref, cot_ref, probs_ref, query_ref, key_ref, value_ref, w_out_ref, w_ref, sums_ref, params_ref, out_ref, back_ref, grad_query_ref, grad_key_ref, grad_value_ref, grad_pooled_ref, key_total, value_total):
    step = pl.program_id(0)
    count = count_ref[2:3, 0:1]
    inside = inside_of(edge_ref[0], pre_ref.shape[0])
    scale, offset, root, root_offset = norm_terms(sums_ref, params_ref, count)
    shift_grad = sums_ref[2:3]
    gain_grad = sums_ref[3:4] * root + shift_grad * root_offset
    slope, shift = back_terms(shift_grad, gain_grad, scale, root, root_offset, count)
    pre = pre_ref[...]
    out_ref[...] = ((pre * scale + offset + mixed_ref[...].astype(full)) * inside).astype(low)
    back = ((cot_ref[...].astype(full) * scale + pre * slope + shift) * inside).astype(low)
    back_ref[...] = back
    grad_attended = dot_cols(back, w_out_ref[...]).astype(low)
    grad_probs = dot_cols(grad_attended, value_ref[...])
    probs = probs_ref[...]
    both = probs * grad_probs
    grad_dots = (
        (both - probs * jnp.sum(both, axis=1, keepdims=True)) * (query_ref.shape[1] ** -0.5)
    ).astype(low)
    grad_query_ref[...] = dot(grad_dots, key_ref[...]).astype(low)
    key_part = dot_rows(grad_dots, query_ref[...])
    value_part = dot_rows(probs.astype(low), grad_attended)

    @pl.when(step == 0)
    def _():
        key_total[...] = key_part
        value_total[...] = value_part

    @pl.when(step != 0)
    def _():
        key_total[...] += key_part
        value_total[...] += value_part

    @pl.when(step == pl.num_programs(0) - 1)
    def _():
        grad_key = key_total[...].astype(low)
        grad_value = value_total[...].astype(low)
        grad_key_ref[...] = grad_key
        grad_value_ref[...] = grad_value
        pooled = dot_cols(grad_key, w_ref[1]) + dot_cols(grad_value, w_ref[2])
        upper = pooled.astype(low)
        lower = (pooled - upper.astype(full)).astype(low)
        for frame in range(FRAMES):
            piece = slice(frame * HALF, (frame + 1) * HALF)
            grad_pooled_ref[2 * frame * HALF : (2 * frame + 1) * HALF, :] = upper[piece, :]
            grad_pooled_ref[(2 * frame + 1) * HALF : (2 * frame + 2) * HALF, :] = lower[piece, :]


def joined_back_kernel(edge_ref, count_ref, hidden_ref, x_ref, cot_ref, grad_query_ref, grad_pooled_ref, w_c_ref, w_theta_ref, sums_c_ref, params_ref, grad_ref, sums_ref):
    count = count_ref[2:3, 0:1]
    inside = inside_of(edge_ref[0], CELLS)
    scale, offset, root, root_offset = norm_terms(sums_c_ref, params_ref, count)
    spread = spread_matrix(CELLS, 2 * HALF, 0.25)
    first = jnp.zeros((1, x_ref.shape[1]), full)
    second = first
    for one in range(hidden_ref.shape[0] // CELLS):
        part = slice(one * CELLS, (one + 1) * CELLS)
        pre = dot(hidden_ref[part, :], w_c_ref[...])
        joined = pre * scale + offset + x_ref[part, :].astype(full)
        grad = cot_ref[part, :].astype(full) + dot_cols(grad_query_ref[part, :], w_theta_ref[0])
        grad += dot(spread, grad_pooled_ref[2 * one * HALF : 2 * (one + 1) * HALF, :])
        grad = grad * inside * gelu_slope(joined)
        grad_ref[part, :] = grad
        first += total(grad)
        second += total(grad * (pre * root + root_offset))
    add_to(sums_ref, 0, first)
    add_to(sums_ref, 1, second)


def expand_back_kernel(edge_ref, count_ref, grad_ref, hidden_ref, pre_b_ref, w_c_ref, sums_c_ref, params_c_ref, back_sums_ref, sums_b_ref, params_b_ref, back_ref, out_ref, sums_ref):
    count = count_ref[2:3, 0:1]
    inside = inside_of(edge_ref[0], grad_ref.shape[0])
    scale, _, root, root_offset = norm_terms(sums_c_ref, params_c_ref, count)
    slope, shift = back_terms(back_sums_ref[0:1], back_sums_ref[1:2], scale, root, root_offset, count)
    pre = dot(hidden_ref[...], w_c_ref[...])
    back = ((grad_ref[...] * scale + pre * slope + shift) * inside).astype(low)
    back_ref[...] = back
    scale, offset, root, root_offset = norm_terms(sums_b_ref, params_b_ref, count)
    pre = pre_b_ref[...]
    grad = dot_cols(back, w_c_ref[...]) * inside * gelu_slope(pre * scale + offset)
    out_ref[...] = grad
    add_to(sums_ref, 0, total(grad))
    add_to(sums_ref, 1, total(grad * (pre * root + root_offset)))


def conv_b_back_kernel(edge_ref, count_ref, grad_ref, pre_b_ref, sums_b_ref, params_b_ref, back_sums_ref, pre_a_ref, sums_a_ref, params_a_ref, w_ref, back_ref, out_ref, sums_ref, wide_ref):
    count = count_ref[2:3, 0:1]
    inside = inside_of(edge_ref[0], CELLS)
    scale, _, root, root_offset = norm_terms(sums_b_ref, params_b_ref, count)
    slope, shift = back_terms(back_sums_ref[0:1], back_sums_ref[1:2], scale, root, root_offset, count)
    scale_a, offset_a, root_a, root_offset_a = norm_terms(sums_a_ref, params_a_ref, count)
    first = jnp.zeros((1, MID), full)
    second = first
    for one in range(grad_ref.shape[0] // CELLS):
        part = slice(one * CELLS, (one + 1) * CELLS)
        back = (grad_ref[part, :] * scale + pre_b_ref[part, :] * slope + shift) * inside
        back_ref[part, :] = back.astype(low)
        wide = wide_ref.at[one]
        spread_taps(back, wide)
        grad = jnp.zeros((CELLS, MID), full)
        for row_step in (-1, 0, 1):
            for col_step in (-1, 0, 1):
                tap = 3 * (row_step + 1) + col_step + 1
                at = GRID - GRID * row_step
                place = 1 - col_step
                grad += dot_cols(
                    wide[at : at + CELLS, place * MID : (place + 1) * MID], w_ref[tap]
                )
        pre = pre_a_ref[part, :]
        grad = grad * inside * gelu_slope(pre * scale_a + offset_a)
        out_ref[part, :] = grad
        first += total(grad)
        second += total(grad * (pre * root_a + root_offset_a))
    add_to(sums_ref, 0, first)
    add_to(sums_ref, 1, second)


def tap_grads_kernel(hidden_ref, back_ref, expand_ref, out_ref, wide_ref, tall_ref):
    step = pl.program_id(0)

    @pl.when(step == 0)
    def _():
        rows = FRAMES * CELLS
        for frame in range(FRAMES):
            part = slice(frame * CELLS, (frame + 1) * CELLS)
            values = hidden_ref[part, :].astype(full)
            for col_step in (-1, 0, 1):
                moved = shift_columns(values, col_step).astype(low)
                wide_ref[col_step + 1, :, part] = moved.T
            back = back_ref[part, :]
            zero = jnp.zeros((GRID, MID), low)
            start = frame * CELLS
            tall_ref[0, start : start + CELLS - GRID, :] = back[GRID:]
            tall_ref[0, start + CELLS - GRID : start + CELLS, :] = zero
            tall_ref[1, part, :] = back
            tall_ref[2, start : start + GRID, :] = zero
            tall_ref[2, start + GRID : start + CELLS, :] = back[: CELLS - GRID]

    for tap in range(9):

        @pl.when(step == tap)
        def _():
            out_ref[0] = dot(wide_ref[tap % 3], tall_ref[tap // 3]).astype(low)

    @pl.when(step >= 9)
    def _():
        out_ref[0] = expand_ref[jnp.maximum(step - 9, 0)]


def frame_grads_kernel(edge_ref, count_ref, grad_ref, pre_ref, sums_a_ref, params_ref, back_sums_ref, turned_ref, rest_ref, back_ref, out_ref):
    step = pl.program_id(0)
    rows = grad_ref.shape[0]

    @pl.when(step == 0)
    def _():
        count = count_ref[2:3, 0:1]
        inside = inside_of(edge_ref[0], CELLS)
        scale, _, root, root_offset = norm_terms(sums_a_ref, params_ref, count)
        slope, shift = back_terms(
            back_sums_ref[0:1], back_sums_ref[1:2], scale, root, root_offset, count
        )
        back_ref[:CELLS, :] = jnp.zeros((CELLS, MID), low)
        back_ref[rows + CELLS :, :] = jnp.zeros((CELLS, MID), low)
        for frame in range(FRAMES):
            part = slice(frame * CELLS, (frame + 1) * CELLS)
            back = (grad_ref[part, :] * scale + pre_ref[part, :] * slope + shift) * inside
            back_ref[(frame + 1) * CELLS : (frame + 2) * CELLS, :] = back.astype(low)

    blocks = turned_ref.shape[0] // MID
    offset = step // blocks
    across = pl.ds(pl.multiple_of((step - offset * blocks) * MID, MID), MID)
    start = pl.multiple_of((2 - offset) * CELLS, CELLS)
    out_ref[0] = dot(turned_ref[across, :], back_ref[pl.ds(start, rows), :]).astype(low)


def input_back_kernel(back_ref, grad_ref, w_ref, out_ref):
    step = pl.program_id(0)
    rows = grad_ref.shape[0]
    grad = grad_ref[...]
    for offset in range(3):
        start = pl.multiple_of(step * rows + (2 - offset) * CELLS, CELLS)
        grad += dot_cols(back_ref[pl.ds(start, rows), :], w_ref[offset])
    out_ref[...] = grad.astype(low)


def on_device(
    clips_in,
    crop_edges,
    cotangent,
    bottle_weights,
    bottle_momentum,
    local_weights,
    local_momentum,
    norm_params,
    norm_momentum,
):
    clip_count, position_count, channels = clips_in.shape
    assert clip_count == 1 and position_count == FRAMES * CELLS
    rows = position_count
    keys = FRAMES * HALF
    x = clips_in.reshape(rows, channels)
    cot = cotangent.reshape(rows, channels)
    edge = (crop_edges, "smem")

    bottle_full = gather_rows(bottle_weights.astype(low).reshape(-1, MID))
    local_low = local_weights.astype(low).reshape(-1, INNER)
    bottle_full, local_low, turned = lax.optimization_barrier((bottle_full, local_low, x.T))
    first = 3 * channels
    second = first + 9 * MID
    weight_a = bottle_full[:first].reshape(3, channels, MID)
    weight_b = bottle_full[first:second].reshape(9, MID, MID)
    weight_c = bottle_full[second:].reshape(MID, channels)
    local_full = lax.all_gather(local_low, AXES, axis=0, tiled=True)
    w_in = local_full[: 3 * channels].reshape(3, channels, INNER)
    w_out = local_full[3 * channels :].reshape(INNER, channels)
    params_a = norm_params[: 2 * MID].reshape(2, MID)
    params_b = norm_params[2 * MID : 4 * MID].reshape(2, MID)
    params_c = norm_params[4 * MID : 4 * MID + 2 * channels].reshape(2, channels)
    params_n = norm_params[4 * MID + 2 * channels :].reshape(2, channels)

    step = 2 * CELLS
    steps = rows // step
    matmul = 2 * rows * MID * channels
    pre_a, part = call(
        conv_a_kernel,
        steps,
        [edge, (x, step), (weight_a, None)],
        [(shape((rows, MID), full), None), (shape((3, MID), full), None)],
        flops=3 * matmul,
        name="conv_a",
    )
    sums_a = sum_devices(part)
    count = (sums_a, None)
    hidden_a, pre_b, part = call(
        conv_b_kernel,
        steps,
        [edge, count, (pre_a, step), (sums_a, None), (params_a, None), (weight_b.reshape(3, 3 * MID, MID), None)],
        [(shape((rows, MID), low), step), (shape((rows, MID), full), step), (shape((2, MID), full), None)],
        [pltpu.VMEM((step // CELLS, CELLS + 2 * GRID, 3 * MID), low)],
        flops=9 * matmul // 4,
        name="conv_b",
    )
    sums_b = sum_devices(part)
    hidden_b, part = call(
        conv_c_kernel,
        steps,
        [edge, count, (pre_b, step), (sums_b, None), (params_b, None), (weight_c, None)],
        [(shape((rows, MID), low), step), (shape((2, channels), full), None)],
        flops=matmul,
        name="conv_c",
    )
    sums_c = sum_devices(part)
    mixed, pooled, query, key_rows, value_rows = call(
        embed_kernel,
        steps,
        [edge, count, (hidden_b, step), (x, step), (sums_c, None), (params_c, None), (weight_c, None), (w_in, None)],
        [
            (shape((rows, channels), low), step),
            (shape((keys, channels), low), step // 4),
            (shape((rows, INNER), low), step),
            (shape((keys, INNER), low), step // 4),
            (shape((keys, INNER), low), step // 4),
        ],
        flops=4 * matmul,
        name="embed",
    )
    probs, attended, pre_w, part = call(
        attend_kernel,
        steps,
        [edge, (query, step), (key_rows, None), (value_rows, None), (w_out, None), (cot, step)],
        [
            (shape((rows, keys), full), step),
            (shape((rows, INNER), low), step),
            (shape((rows, channels), full), step),
            (shape((4, channels), full), None),
        ],
        flops=4 * matmul,
        name="attend",
    )
    sums_n = sum_devices(part)
    clips_out, back_w, grad_query, grad_key, grad_value, grad_pooled = call(
        attend_back_kernel,
        steps,
        [
            edge,
            count,
            (pre_w, step),
            (mixed, step),
            (cot, step),
            (probs, step),
            (query, step),
            (key_rows, None),
            (value_rows, None),
            (w_out, None),
            (w_in, None),
            (sums_n, None),
            (params_n, None),
        ],
        [
            (shape((rows, channels), low), step),
            (shape((rows, channels), low), step),
            (shape((rows, INNER), low), step),
            (shape((keys, INNER), low), None),
            (shape((keys, INNER), low), None),
            (shape((2 * keys, channels), low), None),
        ],
        [pltpu.VMEM((keys, INNER), full), pltpu.VMEM((keys, INNER), full)],
        flops=7 * matmul,
        name="attend_back",
    )
    grad_joined, part = call(
        joined_back_kernel,
        steps,
        [
            edge,
            count,
            (hidden_b, step),
            (x, step),
            (cot, step),
            (grad_query, step),
            (grad_pooled, step // 2),
            (weight_c, None),
            (w_in, None),
            (sums_c, None),
            (params_c, None),
        ],
        [(shape((rows, channels), full), step), (shape((2, channels), full), None)],
        flops=4 * matmul,
        name="joined_back",
    )
    back_sums_c = sum_devices(part)
    grad_theta = dot_rows(mixed, grad_query).astype(low)
    grad_phi = dot_rows(pooled, grad_key).astype(low)
    grad_gather = dot_rows(pooled, grad_value).astype(low)
    grad_w_out = dot_rows(attended, back_w).astype(low)
    local_scatter = Scatter(
        jnp.concatenate(
            [grad_theta, grad_phi, grad_gather, grad_w_out.reshape(2 * INNER, INNER)]
        )
    )
    local_scatter.send()
    back_c, grad_b, part = call(
        expand_back_kernel,
        steps,
        [
            edge,
            count,
            (grad_joined, step),
            (hidden_b, step),
            (pre_b, step),
            (weight_c, None),
            (sums_c, None),
            (params_c, None),
            (back_sums_c, None),
            (sums_b, None),
            (params_b, None),
        ],
        [
            (shape((rows, channels), low), step),
            (shape((rows, MID), full), step),
            (shape((2, MID), full), None),
        ],
        flops=2 * matmul,
        name="expand_back",
    )
    part = local_scatter.after(part)
    local_scatter.send()
    back_sums_b = sum_devices(part)
    grad_weight_c = dot_rows(hidden_b, back_c).astype(low)
    back_b, grad_a, part = call(
        conv_b_back_kernel,
        steps,
        [
            edge,
            count,
            (grad_b, step),
            (pre_b, step),
            (sums_b, None),
            (params_b, None),
            (back_sums_b, None),
            (pre_a, step),
            (sums_a, None),
            (params_a, None),
            (weight_b, None),
        ],
        [
            (shape((rows, MID), low), step),
            (shape((rows, MID), full), step),
            (shape((2, MID), full), None),
        ],
        [pltpu.VMEM((step // CELLS, CELLS + 2 * GRID, 3 * MID), low)],
        flops=9 * matmul // 4,
        name="conv_b_back",
    )
    part = local_scatter.after(part)
    local_scatter.send()
    back_sums_a = sum_devices(part)
    blocks = (first + 9 * MID + channels) // MID
    frame_blocks = first // MID
    (bottle_grads,) = call(
        tap_grads_kernel,
        blocks - frame_blocks,
        [(hidden_a, None), (back_b, None), (grad_weight_c.reshape(-1, MID, MID), None)],
        [(shape((blocks, MID, MID), low), pl.BlockSpec((1, MID, MID), lambda i: (i + frame_blocks, 0, 0)))],
        [pltpu.VMEM((3, MID, rows), low), pltpu.VMEM((3, rows, MID), low)],
        flops=9 * matmul // 4,
        name="tap_grads",
    )
    bottle_grads = local_scatter.after(bottle_grads)
    local_scatter.send()
    padded, bottle_grads = call(
        frame_grads_kernel,
        frame_blocks,
        [
            edge,
            count,
            (grad_a, None),
            (pre_a, None),
            (sums_a, None),
            (params_a, None),
            (back_sums_a, None),
            (turned, None),
            (bottle_grads, pl.BlockSpec(memory_space=pl.ANY)),
        ],
        [
            (shape((rows + 2 * CELLS, MID), low), None),
            (shape((blocks, MID, MID), low), pl.BlockSpec((1, MID, MID), lambda i: (i, 0, 0))),
        ],
        flops=3 * matmul,
        name="frame_grads",
        aliases={8: 1},
    )
    bottle_grads = local_scatter.after(bottle_grads)
    local_scatter.send()
    bottle_shard = Scatter(bottle_grads.reshape(-1, MID)).finish().reshape(-1)
    local_shard = local_scatter.finish().reshape(-1)
    (clips_grad,) = call(
        input_back_kernel,
        steps,
        [(padded, None), (grad_joined, step), (weight_a, None)],
        [(shape((rows, channels), low), step)],
        flops=3 * matmul,
        name="input_back",
    )
    clips_total = clip_count * device_count()
    mean_n, root_n = moments(sums_n, sums_a[2, 0])
    gain_n_grad = root_n[0] * (sums_n[3] - mean_n[0] * sums_n[2])
    norm_grad = jnp.concatenate(
        [
            back_sums_a[1],
            back_sums_a[0],
            back_sums_b[1],
            back_sums_b[0],
            back_sums_c[1],
            back_sums_c[0],
            gain_n_grad,
            sums_n[2],
        ]
    )
    bottle_velocity = (
        momentum_rate * bottle_momentum + bottle_shard / clips_total + decay_rate * bottle_weights
    )
    local_velocity = (
        momentum_rate * local_momentum + local_shard / clips_total + decay_rate * local_weights
    )
    norm_velocity = momentum_rate * norm_momentum + norm_grad / clips_total
    return (
        clips_out.reshape(clips_in.shape),
        clips_grad.reshape(clips_in.shape),
        bottle_weights - learning_rate * bottle_velocity,
        bottle_velocity,
        local_weights - learning_rate * local_velocity,
        local_velocity,
        norm_params - learning_rate * norm_velocity,
        norm_velocity,
    )


def solution(mesh):
    placed = (
        P(("dp", "fsdp"), None, None),
        P(("dp", "fsdp")),
        P(("dp", "fsdp"), None, None),
        P(("dp", "fsdp")),
        P(("dp", "fsdp")),
        P(("dp", "fsdp")),
        P(("dp", "fsdp")),
        P(),
        P(),
    )
    return jax.shard_map(
        on_device,
        mesh=mesh,
        in_specs=placed,
        out_specs=(
            P(("dp", "fsdp"), None, None),
            P(("dp", "fsdp"), None, None),
            P(("dp", "fsdp")),
            P(("dp", "fsdp")),
            P(("dp", "fsdp")),
            P(("dp", "fsdp")),
            P(),
            P(),
        ),
        check_vma=False,
    )
```

```python
import jax
import jax.numpy as jnp
from jax import lax
from jax.experimental import pallas as pl
from jax.experimental.pallas import tpu as pltpu
from jax.sharding import Mesh
from jax.sharding import PartitionSpec as P

MID = 256
INNER = 512
FRAMES = 8
GRID = 16
CELLS = GRID * GRID
HALF = CELLS // 4

epsilon = 1e-05
learning_rate = 0.01
momentum_rate = 0.9
decay_rate = 0.0001
masked_score = -1e30
curve = 0.7978845608028654
cubic = 0.044715

VMEM = 32 * 1024 * 1024
STEP = 2
SHRINK = 10
low = jnp.bfloat16
full = jnp.float32


RINGS = ("dp", "ring")
AXES = RINGS + ("core",)


def device_count():
    return lax.axis_size(AXES)


def device_bit(bit):
    return (lax.axis_index(AXES) >> bit) & 1


def bit_count():
    count = device_count()
    bits = count.bit_length() - 1
    assert count == 1 << bits
    return bits


def swap(values, mask):
    count = device_count()
    return lax.ppermute(values, AXES, [(i, i ^ mask) for i in range(count)])


def sum_devices(values, between=lambda values: values):
    bits = bit_count()
    groups = [[0]]
    low, high = 1, bits - 1
    while low <= high:
        groups.append([low, high] if low < high else [low])
        low, high = low + 1, high - 1
    for number, group in enumerate(groups):
        if number == len(groups) - 1:
            values = between(values)
        if len(group) == 1:
            values = values + swap(values, 1 << group[0])
        else:
            one, two = 1 << group[0], 1 << group[1]
            near, far, both = swap(values, one), swap(values, two), swap(values, one | two)
            values = (values + near) + (far + both)
    return values


def after(values, *others):
    return lax.optimization_barrier((values,) + others)[0]


class Moving:
    def beside(self, other):
        self.got, other = lax.optimization_barrier((self.got, other))
        return other


class Gather(Moving):
    def __init__(self, rows, order):
        self.values, self.order, self.present = rows, list(order), []
        self.tail = rows.shape

    def send(self):
        self.bit = self.order.pop(0)
        self.got = swap(self.values, 1 << self.bit)

    def take(self):
        mine = device_bit(self.bit) == 1
        position = sum(1 for have in self.present if have > self.bit)
        self.values = jnp.stack(
            [jnp.where(mine, self.got, self.values), jnp.where(mine, self.values, self.got)],
            axis=position,
        )
        self.present.append(self.bit)

    def result(self):
        return self.values.reshape((-1,) + self.tail[1:])


class Scatter(Moving):
    def __init__(self, values, order, present):
        self.values = values.reshape((2,) * len(present) + (-1, values.shape[-1]))
        self.present = list(present)
        self.order = list(order)

    def send(self):
        bit = self.order.pop(0)
        position = self.present.index(bit)
        upper = lax.index_in_dim(self.values, 1, position, keepdims=False)
        lower = lax.index_in_dim(self.values, 0, position, keepdims=False)
        mine = device_bit(bit) == 1
        self.keep = jnp.where(mine, upper, lower)
        self.got = swap(jnp.where(mine, lower, upper), 1 << bit)
        self.present.remove(bit)

    def take(self):
        self.values = self.keep.astype(full) + self.got.astype(full)
        if self.present:
            self.values = self.values.astype(low)


class Halves:
    def __init__(self, values, one, two, present):
        width = values.shape[-1] // 2
        self.left = Scatter(values[..., :width], [one, two], present)
        self.right = Scatter(values[..., width:], [two, one], present)

    def send(self):
        self.left.send()
        self.right.send()

    def beside(self, other):
        self.left.got, self.right.got, other = lax.optimization_barrier(
            (self.left.got, self.right.got, other)
        )
        return other

    def take(self):
        self.left.take()
        self.right.take()

    def whole(self, order):
        values = jnp.concatenate([self.left.values, self.right.values], axis=-1)
        return Scatter(values, order, self.left.present)


def dot(left, right):
    return jnp.dot(left, right, preferred_element_type=full)


def dot_cols(left, right):
    return lax.dot_general(left, right, (((1,), (1,)), ((), ())), preferred_element_type=full)


def dot_rows(left, right):
    return lax.dot_general(left, right, (((0,), (0,)), ((), ())), preferred_element_type=full)


def gelu(v):
    return 0.5 * v * (1.0 + jnp.tanh(curve * (v + cubic * (v * v * v))))


def gelu_slope(v):
    square = v * v
    bend = jnp.tanh(v * (curve + (curve * cubic) * square))
    half = 0.5 * v
    return 0.5 + 0.5 * bend + half * (1.0 - bend * bend) * (curve + (3.0 * curve * cubic) * square)


def inside_of(edge, rows):
    cell = lax.broadcasted_iota(jnp.int32, (rows, 1), 0) & (CELLS - 1)
    return (((cell >> 4) < edge) & ((cell & 15) < edge)).astype(full)


def total(values):
    return jnp.sum(values, axis=0, keepdims=True)


def moments(sums_ref, count):
    mean = sums_ref[0:1] / count
    return mean, lax.rsqrt(sums_ref[1:2] / count - mean * mean + epsilon)


def norm_terms(sums_ref, params_ref, count):
    mean, root = moments(sums_ref, count)
    scale = root * params_ref[0:1]
    return scale, params_ref[1:2] - mean * scale, root, -mean * root


def back_terms(shift_grad, gain_grad, scale, root, root_offset, count):
    slope = -(scale * gain_grad * root) / count
    offset = -(scale * (shift_grad + gain_grad * root_offset)) / count
    return slope, offset


def add_to(ref, row, value):
    @pl.when(pl.program_id(0) == 0)
    def _():
        ref[row : row + 1, :] = value

    @pl.when(pl.program_id(0) != 0)
    def _():
        ref[row : row + 1, :] += value


def call(kernel, steps, ins, outs, scratch=(), flops=0, name=None, aliases=None):
    def spec(shape, rows):
        if rows == "smem":
            return pl.BlockSpec(memory_space=pltpu.SMEM)
        if isinstance(rows, pl.BlockSpec):
            return rows
        if rows is None:
            return pl.BlockSpec(shape, lambda i: (0,) * len(shape))
        return pl.BlockSpec((rows,) + tuple(shape[1:]), lambda i: (i,) + (0,) * (len(shape) - 1))

    size = sum(a.size * a.dtype.itemsize for a, _ in ins) + sum(
        a.size * a.dtype.itemsize for a, _ in outs
    )
    return pl.pallas_call(
        kernel,
        grid=(steps,),
        in_specs=[spec(a.shape, rows) for a, rows in ins],
        out_specs=[spec(a.shape, rows) for a, rows in outs],
        out_shape=[a for a, _ in outs],
        scratch_shapes=list(scratch),
        compiler_params=pltpu.CompilerParams(vmem_limit_bytes=VMEM),
        cost_estimate=pl.CostEstimate(
            flops=flops >> SHRINK, bytes_accessed=size >> SHRINK, transcendentals=0
        ),
        input_output_aliases=aliases or {},
        name=name,
    )(*[a for a, _ in ins])


def shape(dims, dtype):
    return jax.ShapeDtypeStruct(dims, dtype)


def conv_a_kernel(edge_ref, x_ref, w_ref, pre_ref, sums_ref):
    step = pl.program_id(0)
    rows = x_ref.shape[0]
    per = rows // CELLS
    steps = FRAMES // per
    for one in range(per):
        frame = step * per + one
        values = x_ref[one * CELLS : (one + 1) * CELLS, :]

        here = pl.ds(pl.multiple_of(frame * CELLS, CELLS), CELLS)
        after = pl.ds(pl.multiple_of((frame + 1) * CELLS, CELLS), CELLS)
        before = pl.ds(pl.multiple_of(jnp.maximum(frame - 1, 0) * CELLS, CELLS), CELLS)
        middle = dot(values, w_ref[1])

        @pl.when(frame == 0)
        def _():
            pre_ref[here, :] = middle

        @pl.when(frame > 0)
        def _():
            pre_ref[here, :] += middle
            pre_ref[before, :] += dot(values, w_ref[2])

        @pl.when(frame < FRAMES - 1)
        def _():
            pre_ref[after, :] = dot(values, w_ref[0])

    @pl.when(step == steps - 1)
    def _():
        edge = edge_ref[0]
        inside = inside_of(edge, CELLS)

        def body(frame, sums):
            v = pre_ref[pl.ds(pl.multiple_of(frame * CELLS, CELLS), CELLS), :]
            m = v * inside
            return sums[0] + total(m), sums[1] + total(m * v)

        zero = jnp.zeros((1, pre_ref.shape[1]), full)
        first, second = lax.fori_loop(0, FRAMES, body, (zero, zero))
        sums_ref[0:1, :] = first
        sums_ref[1:2, :] = second
        sums_ref[2:3, :] = jnp.full(zero.shape, (FRAMES * edge * edge).astype(full))


def shift_columns(values, step):
    if step == 0:
        return values
    rows = values.shape[0]
    column = lax.broadcasted_iota(jnp.int32, (rows, 1), 0) & (GRID - 1)
    edge = GRID - 1 if step == 1 else 0
    moved = pltpu.roll(values, (-step) % rows, 0)
    return jnp.where(column == edge, 0.0, moved)


def spread_taps(values, wide_ref):
    wide_ref[:GRID, :] = jnp.zeros((GRID, 3 * MID), low)
    wide_ref[GRID + CELLS :, :] = jnp.zeros((GRID, 3 * MID), low)
    for step in (-1, 0, 1):
        wide_ref[GRID : GRID + CELLS, (step + 1) * MID : (step + 2) * MID] = shift_columns(
            values, step
        ).astype(low)


def conv_b_kernel(edge_ref, count_ref, pre_ref, sums_a_ref, params_ref, w_ref, hidden_ref, out_ref, sums_ref, wide_ref):
    count = count_ref[2:3, 0:1]
    inside = inside_of(edge_ref[0], CELLS)
    scale, offset, _, _ = norm_terms(sums_a_ref, params_ref, count)
    first = jnp.zeros((1, MID), full)
    second = first
    for one in range(pre_ref.shape[0] // CELLS):
        part = slice(one * CELLS, (one + 1) * CELLS)
        hidden = gelu(pre_ref[part, :] * scale + offset) * inside
        hidden_ref[part, :] = hidden.astype(low)
        wide = wide_ref.at[one]
        spread_taps(hidden, wide)
        values = dot(wide[0:CELLS, :], w_ref[0])
        values += dot(wide[GRID : GRID + CELLS, :], w_ref[1])
        values += dot(wide[2 * GRID : 2 * GRID + CELLS, :], w_ref[2])
        out_ref[part, :] = values
        m = values * inside
        first += total(m)
        second += total(m * values)
    add_to(sums_ref, 0, first)
    add_to(sums_ref, 1, second)


def conv_c_kernel(edge_ref, count_ref, pre_ref, sums_b_ref, params_ref, w_ref, hidden_ref, sums_ref):
    count = count_ref[2:3, 0:1]
    inside = inside_of(edge_ref[0], pre_ref.shape[0])
    scale, offset, _, _ = norm_terms(sums_b_ref, params_ref, count)
    hidden = (gelu(pre_ref[...] * scale + offset) * inside).astype(low)
    hidden_ref[...] = hidden
    values = dot(hidden, w_ref[...])
    add_to(sums_ref, 0, total(values))
    add_to(sums_ref, 1, total(values * values))


def pool_matrix(rows, columns, weight):
    pooled = lax.broadcasted_iota(jnp.int32, (rows, columns), 0) & (HALF - 1)
    cell = lax.broadcasted_iota(jnp.int32, (rows, columns), 1)
    same = ((cell >> 5) == (pooled >> 3)) & (((cell >> 1) & 7) == (pooled & 7))
    return jnp.where(same, weight, 0.0).astype(low)


def spread_matrix(rows, columns, weight):
    cell = lax.broadcasted_iota(jnp.int32, (rows, columns), 0)
    pooled = lax.broadcasted_iota(jnp.int32, (rows, columns), 1) & (HALF - 1)
    same = ((cell >> 5) == (pooled >> 3)) & (((cell >> 1) & 7) == (pooled & 7))
    return jnp.where(same, weight, 0.0).astype(low)


def embed_kernel(edge_ref, count_ref, hidden_ref, x_ref, sums_c_ref, params_ref, w_c_ref, w_ref, mixed_ref, pooled_ref, query_ref, key_ref, value_ref):
    count = count_ref[2:3, 0:1]
    inside = inside_of(edge_ref[0], CELLS)
    scale, offset, _, _ = norm_terms(sums_c_ref, params_ref, count)
    pool = pool_matrix(HALF, CELLS, 0.25)
    for one in range(hidden_ref.shape[0] // CELLS):
        part = slice(one * CELLS, (one + 1) * CELLS)
        piece = slice(one * HALF, (one + 1) * HALF)
        joined = dot(hidden_ref[part, :], w_c_ref[...]) * scale + offset + x_ref[part, :].astype(full)
        mixed = (gelu(joined) * inside).astype(low)
        mixed_ref[part, :] = mixed
        query_ref[part, :] = dot(mixed, w_ref[0]).astype(low)
        pooled = dot(pool, mixed).astype(low)
        pooled_ref[piece, :] = pooled
        key_ref[piece, :] = dot(pooled, w_ref[1]).astype(low)
        value_ref[piece, :] = dot(pooled, w_ref[2]).astype(low)


def attend_kernel(edge_ref, query_ref, key_ref, value_ref, w_out_ref, cot_ref, probs_ref, attended_ref, pre_ref, sums_ref):
    edge = edge_ref[0]
    rows = query_ref.shape[0]
    inside = inside_of(edge, rows)
    keys = key_ref.shape[0]
    spot = lax.broadcasted_iota(jnp.int32, (1, keys), 1)
    keyed = (((spot >> 3) & 7) * 2 < edge) & ((spot & 7) * 2 < edge)
    scores = dot_cols(query_ref[...], key_ref[...]) * (query_ref.shape[1] ** -0.5)
    scores = jnp.where(keyed, scores, masked_score)
    weights = jnp.exp(scores - jnp.max(scores, axis=1, keepdims=True))
    probs = weights * (inside / jnp.sum(weights, axis=1, keepdims=True))
    probs = probs.astype(low)
    probs_ref[...] = probs
    attended = dot(probs, value_ref[...]).astype(low)
    attended_ref[...] = attended
    values = dot(attended, w_out_ref[...])
    pre_ref[...] = values.astype(low)
    upstream = cot_ref[...].astype(full) * inside
    add_to(sums_ref, 0, total(values))
    add_to(sums_ref, 1, total(values * values))
    add_to(sums_ref, 2, total(upstream))
    add_to(sums_ref, 3, total(upstream * values))


def attend_back_kernel(edge_ref, count_ref, pre_ref, mixed_ref, cot_ref, probs_ref, query_ref, key_ref, value_ref, w_out_ref, w_ref, sums_ref, params_ref, out_ref, back_ref, grad_query_ref, grad_key_ref, grad_value_ref, grad_pooled_ref, key_total, value_total):
    step = pl.program_id(0)
    count = count_ref[2:3, 0:1]
    inside = inside_of(edge_ref[0], pre_ref.shape[0])
    scale, offset, root, root_offset = norm_terms(sums_ref, params_ref, count)
    shift_grad = sums_ref[2:3]
    gain_grad = sums_ref[3:4] * root + shift_grad * root_offset
    slope, shift = back_terms(shift_grad, gain_grad, scale, root, root_offset, count)
    pre = pre_ref[...].astype(full)
    out_ref[...] = ((pre * scale + offset + mixed_ref[...].astype(full)) * inside).astype(low)
    back = ((cot_ref[...].astype(full) * scale + pre * slope + shift) * inside).astype(low)
    back_ref[...] = back
    grad_attended = dot_cols(back, w_out_ref[...]).astype(low)
    grad_probs = dot_cols(grad_attended, value_ref[...])
    probs_low = probs_ref[...]
    probs = probs_low.astype(full)
    both = probs * grad_probs
    grad_dots = (
        (both - probs * jnp.sum(both, axis=1, keepdims=True)) * (query_ref.shape[1] ** -0.5)
    ).astype(low)
    grad_query_ref[...] = dot(grad_dots, key_ref[...]).astype(low)
    key_part = dot_rows(grad_dots, query_ref[...])
    value_part = dot_rows(probs_low, grad_attended)

    @pl.when(step == 0)
    def _():
        key_total[...] = key_part
        value_total[...] = value_part

    @pl.when(step != 0)
    def _():
        key_total[...] += key_part
        value_total[...] += value_part

    @pl.when(step == pl.num_programs(0) - 1)
    def _():
        grad_key = key_total[...].astype(low)
        grad_value = value_total[...].astype(low)
        grad_key_ref[...] = grad_key
        grad_value_ref[...] = grad_value
        pooled = dot_cols(grad_key, w_ref[1]) + dot_cols(grad_value, w_ref[2])
        upper = pooled.astype(low)
        lower = (pooled - upper.astype(full)).astype(low)
        for frame in range(FRAMES):
            piece = slice(frame * HALF, (frame + 1) * HALF)
            grad_pooled_ref[2 * frame * HALF : (2 * frame + 1) * HALF, :] = upper[piece, :]
            grad_pooled_ref[(2 * frame + 1) * HALF : (2 * frame + 2) * HALF, :] = lower[piece, :]


def local_grads_kernel(mixed_ref, grad_query_ref, pooled_ref, grad_key_ref, grad_value_ref, attended_ref, back_ref, out_ref):
    step = pl.program_id(0)
    rows = out_ref.shape[2]

    def put(grads):
        for shard in range(grads.shape[0] // rows):
            out_ref[shard % 2, shard // 2] = grads[shard * rows : (shard + 1) * rows, :]

    @pl.when(step < 2)
    def _():
        put(dot_rows(mixed_ref[...], grad_query_ref[...]).astype(low))

    @pl.when((step >= 2) & (step < 4))
    def _():
        put(dot_rows(pooled_ref[...], grad_key_ref[...]).astype(low))

    @pl.when((step >= 4) & (step < 6))
    def _():
        put(dot_rows(pooled_ref[...], grad_value_ref[...]).astype(low))

    @pl.when(step >= 6)
    def _():
        grads = dot_rows(attended_ref[...], back_ref[...]).astype(low)
        half = rows // 2
        for shard in range(grads.shape[0] // half):
            part = grads[shard * half : (shard + 1) * half, :]
            out_ref[shard % 2, shard // 2, :half, :] = part[:, :INNER]
            out_ref[shard % 2, shard // 2, half:, :] = part[:, INNER:]


def joined_back_kernel(edge_ref, count_ref, hidden_ref, x_ref, cot_ref, grad_query_ref, grad_pooled_ref, w_c_ref, w_theta_ref, sums_c_ref, params_ref, grad_ref, sums_ref):
    count = count_ref[2:3, 0:1]
    inside = inside_of(edge_ref[0], CELLS)
    scale, offset, root, root_offset = norm_terms(sums_c_ref, params_ref, count)
    spread = spread_matrix(CELLS, 2 * HALF, 0.25)
    first = jnp.zeros((1, x_ref.shape[1]), full)
    second = first
    for one in range(hidden_ref.shape[0] // CELLS):
        part = slice(one * CELLS, (one + 1) * CELLS)
        pre = dot(hidden_ref[part, :], w_c_ref[...])
        joined = pre * scale + offset + x_ref[part, :].astype(full)
        grad = cot_ref[part, :].astype(full) + dot_cols(grad_query_ref[part, :], w_theta_ref[0])
        grad += dot(spread, grad_pooled_ref[2 * one * HALF : 2 * (one + 1) * HALF, :])
        grad = grad * inside * gelu_slope(joined)
        grad_ref[part, :] = grad.astype(low)
        first += total(grad)
        second += total(grad * (pre * root + root_offset))
    add_to(sums_ref, 0, first)
    add_to(sums_ref, 1, second)


def expand_back_kernel(edge_ref, count_ref, grad_ref, hidden_ref, pre_b_ref, w_c_ref, sums_c_ref, params_c_ref, back_sums_ref, sums_b_ref, params_b_ref, back_ref, out_ref, sums_ref):
    count = count_ref[2:3, 0:1]
    inside = inside_of(edge_ref[0], grad_ref.shape[0])
    scale, _, root, root_offset = norm_terms(sums_c_ref, params_c_ref, count)
    slope, shift = back_terms(back_sums_ref[0:1], back_sums_ref[1:2], scale, root, root_offset, count)
    pre = dot(hidden_ref[...], w_c_ref[...])
    back = ((grad_ref[...].astype(full) * scale + pre * slope + shift) * inside).astype(low)
    back_ref[...] = back
    scale, offset, root, root_offset = norm_terms(sums_b_ref, params_b_ref, count)
    pre = pre_b_ref[...]
    grad = dot_cols(back, w_c_ref[...]) * inside * gelu_slope(pre * scale + offset)
    out_ref[...] = grad
    add_to(sums_ref, 0, total(grad))
    add_to(sums_ref, 1, total(grad * (pre * root + root_offset)))


def conv_b_back_kernel(edge_ref, count_ref, grad_ref, pre_b_ref, sums_b_ref, params_b_ref, back_sums_ref, pre_a_ref, sums_a_ref, params_a_ref, w_ref, back_ref, out_ref, sums_ref, wide_ref):
    count = count_ref[2:3, 0:1]
    inside = inside_of(edge_ref[0], CELLS)
    scale, _, root, root_offset = norm_terms(sums_b_ref, params_b_ref, count)
    slope, shift = back_terms(back_sums_ref[0:1], back_sums_ref[1:2], scale, root, root_offset, count)
    scale_a, offset_a, root_a, root_offset_a = norm_terms(sums_a_ref, params_a_ref, count)
    first = jnp.zeros((1, MID), full)
    second = first
    for one in range(grad_ref.shape[0] // CELLS):
        part = slice(one * CELLS, (one + 1) * CELLS)
        back = (grad_ref[part, :] * scale + pre_b_ref[part, :] * slope + shift) * inside
        back_ref[part, :] = back.astype(low)
        wide = wide_ref.at[one]
        spread_taps(back, wide)
        grad = jnp.zeros((CELLS, MID), full)
        for row_step in (-1, 0, 1):
            for col_step in (-1, 0, 1):
                tap = 3 * (row_step + 1) + col_step + 1
                at = GRID - GRID * row_step
                place = 1 - col_step
                grad += dot_cols(
                    wide[at : at + CELLS, place * MID : (place + 1) * MID], w_ref[tap]
                )
        pre = pre_a_ref[part, :]
        grad = grad * inside * gelu_slope(pre * scale_a + offset_a)
        out_ref[part, :] = grad
        first += total(grad)
        second += total(grad * (pre * root_a + root_offset_a))
    add_to(sums_ref, 0, first)
    add_to(sums_ref, 1, second)


def tap_grads_kernel(hidden_ref, back_ref, expand_ref, near_ref, far_ref, wide_ref, tall_ref):
    near = near_ref.shape[0]
    step = pl.program_id(0)

    @pl.when(step == 0)
    def _():
        rows = FRAMES * CELLS
        for frame in range(FRAMES):
            part = slice(frame * CELLS, (frame + 1) * CELLS)
            values = hidden_ref[part, :].astype(full)
            for col_step in (-1, 0, 1):
                moved = shift_columns(values, col_step).astype(low)
                wide_ref[col_step + 1, :, part] = moved.T
            back = back_ref[part, :]
            zero = jnp.zeros((GRID, MID), low)
            start = frame * CELLS
            tall_ref[0, start : start + CELLS - GRID, :] = back[GRID:]
            tall_ref[0, start + CELLS - GRID : start + CELLS, :] = zero
            tall_ref[1, part, :] = back
            tall_ref[2, start : start + GRID, :] = zero
            tall_ref[2, start + GRID : start + CELLS, :] = back[: CELLS - GRID]

    for tap in range(9):

        @pl.when(step == tap)
        def _():
            grads = dot(wide_ref[tap % 3], tall_ref[tap // 3]).astype(low)
            start = tap * MID - near
            if start < 0:
                near_ref[...] = grads[:near]
                far_ref[: MID - near, :] = grads[near:]
            else:
                far_ref[start : start + MID, :] = grads

    @pl.when(step == pl.num_programs(0) - 1)
    def _():
        far_ref[9 * MID - near :, :] = expand_ref[...]


def frame_grads_kernel(edge_ref, count_ref, grad_ref, pre_ref, sums_a_ref, params_ref, back_sums_ref, turned_ref, rest_ref, back_ref, out_ref):
    step = pl.program_id(0)
    rows = grad_ref.shape[0]

    @pl.when(step == 0)
    def _():
        count = count_ref[2:3, 0:1]
        inside = inside_of(edge_ref[0], CELLS)
        scale, _, root, root_offset = norm_terms(sums_a_ref, params_ref, count)
        slope, shift = back_terms(
            back_sums_ref[0:1], back_sums_ref[1:2], scale, root, root_offset, count
        )
        back_ref[:CELLS, :] = jnp.zeros((CELLS, MID), low)
        back_ref[rows + CELLS :, :] = jnp.zeros((CELLS, MID), low)
        for frame in range(FRAMES):
            part = slice(frame * CELLS, (frame + 1) * CELLS)
            back = (grad_ref[part, :] * scale + pre_ref[part, :] * slope + shift) * inside
            back_ref[(frame + 1) * CELLS : (frame + 2) * CELLS, :] = back.astype(low)

    blocks = turned_ref.shape[0] // MID
    offset = step // blocks
    across = pl.ds(pl.multiple_of((step - offset * blocks) * MID, MID), MID)
    start = pl.multiple_of((2 - offset) * CELLS, CELLS)
    place = pl.ds(pl.multiple_of(step * MID, MID), MID)
    out_ref[place, :] = dot(turned_ref[across, :], back_ref[pl.ds(start, rows), :]).astype(low)

    @pl.when(step == pl.num_programs(0) - 1)
    def _():
        out_ref[pl.num_programs(0) * MID :, :] = rest_ref[...]


def input_back_kernel(back_ref, grad_ref, w_ref, out_ref):
    step = pl.program_id(0)
    rows = grad_ref.shape[0]
    grad = grad_ref[...].astype(full)
    for offset in range(3):
        start = pl.multiple_of(step * rows + (2 - offset) * CELLS, CELLS)
        grad += dot_cols(back_ref[pl.ds(start, rows), :], w_ref[offset])
    out_ref[...] = grad.astype(low)


def on_device(
    clips_in,
    crop_edges,
    cotangent,
    bottle_weights,
    bottle_momentum,
    local_weights,
    local_momentum,
    norm_params,
    norm_momentum,
):
    clip_count, position_count, channels = clips_in.shape
    assert clip_count == 1 and position_count == FRAMES * CELLS
    rows = position_count
    keys = FRAMES * HALF
    x = clips_in.reshape(rows, channels)
    cot = cotangent.reshape(rows, channels)
    edge = (crop_edges, "smem")

    bits = bit_count()
    top = bits - 1
    inner = list(range(top - 1, -1, -1))
    mine = bottle_weights.astype(low).reshape(-1, MID)
    other = swap(mine, 1 << top)
    high = device_bit(top) == 1
    near = Gather(jnp.where(high, other, mine), inner)
    far = Gather(jnp.where(high, mine, other), inner)
    local_low = local_weights.astype(low).reshape(-1, INNER)
    turned = x.T
    for number in range(len(inner)):
        near.send()
        if number > 0:
            far.values = after(far.values, near.values)
            far.send()
        if 0 < number < len(inner) - 1:
            near.got = far.beside(near.got)
        if number == len(inner) - 2:
            near.got, turned, local_low = lax.optimization_barrier((near.got, turned, local_low))
        near.take()
        if 0 < number < len(inner) - 1:
            far.take()
    near_full = near.result()
    local_low = after(local_low, near_full)
    local_full = lax.all_gather(local_low, AXES, axis=0, tiled=True)
    first = 3 * channels
    weight_a = near_full[:first].reshape(3, channels, MID)
    w_in = local_full[: 3 * channels].reshape(3, channels, INNER)
    w_out = local_full[3 * channels :].reshape(INNER, channels)
    params_a = norm_params[: 2 * MID].reshape(2, MID)
    params_b = norm_params[2 * MID : 4 * MID].reshape(2, MID)
    params_c = norm_params[4 * MID : 4 * MID + 2 * channels].reshape(2, channels)
    params_n = norm_params[4 * MID + 2 * channels :].reshape(2, channels)

    step = STEP * CELLS
    steps = rows // step
    matmul = 2 * rows * MID * channels
    pre_a, part = call(
        conv_a_kernel,
        steps,
        [edge, (x, step), (weight_a, None)],
        [(shape((rows, MID), full), None), (shape((3, MID), full), None)],
        flops=3 * matmul,
        name="conv_a",
    )
    part = far.beside(part)
    far.take()
    far.send()
    sums_a = far.beside(sum_devices(part))
    far.take()
    far_full = far.result()
    rest = first + 9 * MID - near_full.shape[0]
    weight_b = jnp.concatenate([near_full[first:], far_full[:rest]])
    weight_c = far_full[rest:].reshape(MID, channels)
    count = (sums_a, None)
    hidden_a, pre_b, part = call(
        conv_b_kernel,
        steps,
        [edge, count, (pre_a, step), (sums_a, None), (params_a, None), (weight_b.reshape(3, 3 * MID, MID), None)],
        [(shape((rows, MID), low), step), (shape((rows, MID), full), step), (shape((2, MID), full), None)],
        [pltpu.VMEM((step // CELLS, CELLS + 2 * GRID, 3 * MID), low)],
        flops=9 * matmul // 4,
        name="conv_b",
    )
    sums_b = sum_devices(part)
    hidden_b, part = call(
        conv_c_kernel,
        steps,
        [edge, count, (pre_b, step), (sums_b, None), (params_b, None), (weight_c, None)],
        [(shape((rows, MID), low), step), (shape((2, channels), full), None)],
        flops=matmul,
        name="conv_c",
    )
    sums_c = sum_devices(part)
    mixed, pooled, query, key_rows, value_rows = call(
        embed_kernel,
        steps,
        [edge, count, (hidden_b, step), (x, step), (sums_c, None), (params_c, None), (weight_c, None), (w_in, None)],
        [
            (shape((rows, channels), low), step),
            (shape((keys, channels), low), step // 4),
            (shape((rows, INNER), low), step),
            (shape((keys, INNER), low), step // 4),
            (shape((keys, INNER), low), step // 4),
        ],
        flops=4 * matmul,
        name="embed",
    )
    probs, attended, pre_w, part = call(
        attend_kernel,
        steps,
        [edge, (query, step), (key_rows, None), (value_rows, None), (w_out, None), (cot, step)],
        [
            (shape((rows, keys), low), step),
            (shape((rows, INNER), low), step),
            (shape((rows, channels), low), step),
            (shape((4, channels), full), None),
        ],
        flops=4 * matmul,
        name="attend",
    )
    sums_n = sum_devices(part)
    clips_out, back_w, grad_query, grad_key, grad_value, grad_pooled = call(
        attend_back_kernel,
        steps,
        [
            edge,
            count,
            (pre_w, step),
            (mixed, step),
            (cot, step),
            (probs, step),
            (query, step),
            (key_rows, None),
            (value_rows, None),
            (w_out, None),
            (w_in, None),
            (sums_n, None),
            (params_n, None),
        ],
        [
            (shape((rows, channels), low), step),
            (shape((rows, channels), low), step),
            (shape((rows, INNER), low), step),
            (shape((keys, INNER), low), None),
            (shape((keys, INNER), low), None),
            (shape((2 * keys, channels), low), None),
        ],
        [pltpu.VMEM((keys, INNER), full), pltpu.VMEM((keys, INNER), full)],
        flops=7 * matmul,
        name="attend_back",
    )
    shard_rows = local_low.shape[0]
    pairs = device_count() // 2
    if shard_rows % 32 == 0:

        def columns(width, at):
            return pl.BlockSpec((rows, width), lambda i: (0, at(i)))

        (local_grads,) = call(
            local_grads_kernel,
            8,
            [
                (mixed, columns(2 * MID, lambda i: jnp.minimum(i, 1))),
                (grad_query, None),
                (pooled, pl.BlockSpec((keys, 2 * MID), lambda i: (0, i & 1))),
                (grad_key, None),
                (grad_value, None),
                (attended, columns(MID, lambda i: jnp.maximum(i - 6, 0))),
                (back_w, None),
            ],
            [
                (
                    shape((2, pairs, shard_rows, INNER), low),
                    pl.BlockSpec((2, pairs // 8, shard_rows, INNER), lambda i: (0, i, 0, 0)),
                )
            ],
            flops=5 * matmul,
            name="local_grads",
        )
    else:
        grad_out = dot_rows(attended, back_w).astype(low)
        grad_out = grad_out.reshape(-1, shard_rows // 2, 2, INNER).transpose(0, 2, 1, 3)
        local_grads = jnp.concatenate(
            [
                dot_rows(mixed, grad_query).astype(low),
                dot_rows(pooled, grad_key).astype(low),
                dot_rows(pooled, grad_value).astype(low),
                grad_out.reshape(-1, INNER),
            ]
        )
        local_grads = local_grads.reshape(pairs, 2, shard_rows, INNER).transpose(1, 0, 2, 3)
    spans = list(range(top, 0, -1))
    local = Scatter(local_grads, [0], [0] + spans)
    local.send()
    grad_query = local.beside(grad_query)
    local.take()
    local = Halves(local.values, 1, top, spans)
    local.send()
    grad_joined, part = call(
        joined_back_kernel,
        steps,
        [
            edge,
            count,
            (hidden_b, step),
            (x, step),
            (cot, step),
            (grad_query, step),
            (grad_pooled, step // 2),
            (weight_c, None),
            (w_in, None),
            (sums_c, None),
            (params_c, None),
        ],
        [(shape((rows, channels), low), step), (shape((2, channels), full), None)],
        flops=4 * matmul,
        name="joined_back",
    )
    part = local.beside(part)
    local.take()
    local.send()
    back_sums_c = local.beside(sum_devices(part))
    local.take()
    local = local.whole(range(2, top))
    local.send()
    back_c, grad_b, part = call(
        expand_back_kernel,
        steps,
        [
            edge,
            count,
            (grad_joined, step),
            (hidden_b, step),
            (pre_b, step),
            (weight_c, None),
            (sums_c, None),
            (params_c, None),
            (back_sums_c, None),
            (sums_b, None),
            (params_b, None),
        ],
        [
            (shape((rows, channels), low), step),
            (shape((rows, MID), full), step),
            (shape((2, MID), full), None),
        ],
        flops=2 * matmul,
        name="expand_back",
    )
    back_sums_b = local.beside(sum_devices(part))
    local.take()
    local.send()
    grad_weight_c = dot_rows(hidden_b, back_c).astype(low)
    back_b, grad_a, part = call(
        conv_b_back_kernel,
        steps,
        [
            edge,
            count,
            (grad_b, step),
            (pre_b, step),
            (sums_b, None),
            (params_b, None),
            (back_sums_b, None),
            (pre_a, step),
            (sums_a, None),
            (params_a, None),
            (weight_b.reshape(9, MID, MID), None),
        ],
        [
            (shape((rows, MID), low), step),
            (shape((rows, MID), full), step),
            (shape((2, MID), full), None),
        ],
        [pltpu.VMEM((step // CELLS, CELLS + 2 * GRID, 3 * MID), low)],
        flops=9 * matmul // 4,
        name="conv_b_back",
    )
    half = near_full.shape[0]
    near_grads, far_grads = call(
        tap_grads_kernel,
        10,
        [(hidden_a, None), (back_b, None), (grad_weight_c.reshape(-1, MID), None)],
        [(shape((half - first, MID), low), None), (shape((half, MID), low), None)],
        [pltpu.VMEM((3, MID, rows), low), pltpu.VMEM((3, rows, MID), low)],
        flops=9 * matmul // 4,
        name="tap_grads",
    )
    part = local.beside(part)
    local.take()
    while local.order:
        local.send()
        local.take()
    spans = list(range(top - 1, 0, -1))
    far = Scatter(far_grads, [0], spans + [0])
    far.send()
    back_sums_a = sum_devices(part, far.beside)
    far.take()
    far = Halves(far.values, 1, 2, spans)
    far.send()
    padded, near_grads = call(
        frame_grads_kernel,
        first // MID,
        [
            edge,
            count,
            (grad_a, None),
            (pre_a, None),
            (sums_a, None),
            (params_a, None),
            (back_sums_a, None),
            (turned, None),
            (near_grads, None),
        ],
        [(shape((rows + 2 * CELLS, MID), low), None), (shape((half, MID), low), None)],
        flops=3 * matmul,
        name="frame_grads",
    )
    near_grads = far.beside(near_grads)
    near = Scatter(near_grads, [0], spans + [0])
    near.send()
    far.take()
    far.send()
    padded = near.beside(padded)
    near.take()
    near = Halves(near.values, 1, 2, spans)
    near.send()
    (clips_grad,) = call(
        input_back_kernel,
        steps,
        [(padded, None), (grad_joined, step), (weight_a, None)],
        [(shape((rows, channels), low), step)],
        flops=3 * matmul,
        name="input_back",
    )
    clips_grad = near.beside(far.beside(clips_grad))
    near.take()
    near.send()
    far.take()
    far = far.whole(range(3, top))
    while far.order:
        far.send()
        far.take()
    near.take()
    near = near.whole(range(3, top))
    while near.order:
        near.send()
        near.take()
    near_sum, far_sum = near.values, far.values
    got = swap(jnp.where(high, near_sum, far_sum).astype(low), 1 << top)
    bottle_shard = (jnp.where(high, far_sum, near_sum) + got.astype(full)).reshape(-1)
    local_sum = local.values.astype(full)
    halves = local_sum.reshape(2, -1, INNER)
    joint = jnp.concatenate([halves[0], halves[1]], axis=1).reshape(-1)
    in_out = lax.axis_index(AXES) * shard_rows >= 3 * channels
    local_shard = jnp.where(in_out, joint, local_sum.reshape(-1))
    clips_total = clip_count * device_count()
    mean_n, root_n = moments(sums_n, sums_a[2, 0])
    gain_n_grad = root_n[0] * (sums_n[3] - mean_n[0] * sums_n[2])
    norm_grad = jnp.concatenate(
        [
            back_sums_a[1],
            back_sums_a[0],
            back_sums_b[1],
            back_sums_b[0],
            back_sums_c[1],
            back_sums_c[0],
            gain_n_grad,
            sums_n[2],
        ]
    )
    bottle_velocity = (
        momentum_rate * bottle_momentum + bottle_shard / clips_total + decay_rate * bottle_weights
    )
    local_velocity = (
        momentum_rate * local_momentum + local_shard / clips_total + decay_rate * local_weights
    )
    norm_velocity = momentum_rate * norm_momentum + norm_grad / clips_total
    return (
        clips_out.reshape(clips_in.shape),
        clips_grad.reshape(clips_in.shape),
        bottle_weights - learning_rate * bottle_velocity,
        bottle_velocity,
        local_weights - learning_rate * local_velocity,
        local_velocity,
        norm_params - learning_rate * norm_velocity,
        norm_velocity,
    )


def solution(mesh):
    devices = mesh.devices.reshape(mesh.shape["dp"], mesh.shape["fsdp"] // 2, 2)
    split = P(AXES)
    return jax.shard_map(
        on_device,
        mesh=Mesh(devices, AXES),
        in_specs=(split,) * 7 + (P(),) * 2,
        out_specs=(split,) * 6 + (P(),) * 2,
        check_vma=False,
    )
```

```python
import math

import jax
import jax.numpy as jnp
from jax import lax
from jax.experimental import pallas as pl
from jax.experimental.pallas import tpu as pltpu
from jax.sharding import Mesh
from jax.sharding import PartitionSpec as P

MID = 256
INNER = 512
FRAMES = 8
GRID = 16
CELLS = GRID * GRID
HALF = CELLS // 4

epsilon = 1e-05
learning_rate = 0.01
momentum_rate = 0.9
decay_rate = 0.0001
masked_score = -1e30
curve = 0.7978845608028654
cubic = 0.044715

VMEM = 32 * 1024 * 1024
STEP = 2
SHRINK = 10
FAR = 1
WHOLE = 3
PAIRS = 3
low = jnp.bfloat16
full = jnp.float32


RINGS = ("dp", "ring")
AXES = RINGS + ("core",)


def device_count():
    return lax.axis_size(AXES)


def device_bit(bit):
    return (lax.axis_index(AXES) >> bit) & 1


def bit_count():
    count = device_count()
    bits = count.bit_length() - 1
    assert count == 1 << bits
    return bits


def swap(values, mask):
    count = device_count()
    return lax.ppermute(values, AXES, [(i, i ^ mask) for i in range(count)])


def sum_devices(values, between=lambda values: values):
    bits = bit_count()
    groups = [[0]]
    low, high = 1, bits - 1
    while low <= high:
        groups.append([low, high] if low < high else [low])
        low, high = low + 1, high - 1
    for number, group in enumerate(groups):
        if number == len(groups) - 1:
            values = between(values)
        if len(group) == 1:
            values = values + swap(values, 1 << group[0])
        else:
            one, two = 1 << group[0], 1 << group[1]
            near, far, both = swap(values, one), swap(values, two), swap(values, one | two)
            values = (values + near) + (far + both)
    return values


def after(values, *others):
    return lax.optimization_barrier((values,) + others)[0]


def sum_small(values, axes=AXES):
    copies = jnp.broadcast_to(values[None], (lax.axis_size(axes),) + values.shape)
    return jnp.sum(lax.all_to_all(copies, axes, 0, 0), axis=0)


def sum_pairs(values):
    return sum_small(values + swap(values, 1), RINGS)


class Moving:
    def beside(self, other):
        self.got, other = lax.optimization_barrier((self.got, other))
        return other


class Gather(Moving):
    def __init__(self, rows, order):
        self.values, self.order, self.present = rows, list(order), []
        self.tail = rows.shape

    def send(self):
        self.bit = self.order.pop(0)
        self.got = swap(self.values, 1 << self.bit)

    def take(self):
        mine = device_bit(self.bit) == 1
        position = sum(1 for have in self.present if have > self.bit)
        self.values = jnp.stack(
            [jnp.where(mine, self.got, self.values), jnp.where(mine, self.values, self.got)],
            axis=position,
        )
        self.present.append(self.bit)

    def result(self):
        return self.values.reshape((-1,) + self.tail[1:])


class Scatter(Moving):
    def __init__(self, values, order, present):
        self.values = values.reshape((2,) * len(present) + (-1, values.shape[-1]))
        self.present = list(present)
        self.order = list(order)

    def send(self):
        bit = self.order.pop(0)
        position = self.present.index(bit)
        upper = lax.index_in_dim(self.values, 1, position, keepdims=False)
        lower = lax.index_in_dim(self.values, 0, position, keepdims=False)
        mine = device_bit(bit) == 1
        self.keep = jnp.where(mine, upper, lower)
        self.got = swap(jnp.where(mine, lower, upper), 1 << bit)
        self.present.remove(bit)

    def take(self):
        self.values = self.keep.astype(full) + self.got.astype(full)
        if self.present:
            self.values = self.values.astype(low)


class Halves:
    def __init__(self, values, one, two, present):
        width = values.shape[-1] // 2
        self.left = Scatter(values[..., :width], [one, two], present)
        self.right = Scatter(values[..., width:], [two, one], present)

    def send(self):
        self.left.send()
        self.right.send()

    def beside(self, other):
        self.left.got, self.right.got, other = lax.optimization_barrier(
            (self.left.got, self.right.got, other)
        )
        return other

    def take(self):
        self.left.take()
        self.right.take()

    def whole(self, order):
        values = jnp.concatenate([self.left.values, self.right.values], axis=-1)
        return Scatter(values, order, self.left.present)


def dot(left, right):
    return jnp.dot(left, right, preferred_element_type=full)


def dot_cols(left, right):
    return lax.dot_general(left, right, (((1,), (1,)), ((), ())), preferred_element_type=full)


def dot_rows(left, right):
    return lax.dot_general(left, right, (((0,), (0,)), ((), ())), preferred_element_type=full)


def gelu(v):
    return 0.5 * v * (1.0 + jnp.tanh(curve * (v + cubic * (v * v * v))))


def gelu_slope(v):
    square = v * v
    bend = jnp.tanh(v * (curve + (curve * cubic) * square))
    half = 0.5 * v
    return 0.5 + 0.5 * bend + half * (1.0 - bend * bend) * (curve + (3.0 * curve * cubic) * square)


def inside_of(edge, rows):
    cell = lax.broadcasted_iota(jnp.int32, (rows, 1), 0) & (CELLS - 1)
    return (((cell >> 4) < edge) & ((cell & 15) < edge)).astype(full)


def total(values):
    return jnp.sum(values, axis=0, keepdims=True)


def moments(sums_ref, count):
    mean = sums_ref[0:1] / count
    return mean, lax.rsqrt(sums_ref[1:2] / count - mean * mean + epsilon)


def norm_terms(sums_ref, params_ref, count):
    mean, root = moments(sums_ref, count)
    scale = root * params_ref[0:1]
    return scale, params_ref[1:2] - mean * scale, root, -mean * root


def back_terms(shift_grad, gain_grad, scale, root, root_offset, count):
    slope = -(scale * gain_grad * root) / count
    offset = -(scale * (shift_grad + gain_grad * root_offset)) / count
    return slope, offset


def add_to(ref, row, value):
    @pl.when(pl.program_id(0) == 0)
    def _():
        ref[row : row + 1, :] = value

    @pl.when(pl.program_id(0) != 0)
    def _():
        ref[row : row + 1, :] += value


def call(kernel, steps, ins, outs, scratch=(), flops=0, name=None, aliases=None):
    def spec(shape, rows):
        if rows == "smem":
            return pl.BlockSpec(memory_space=pltpu.SMEM)
        if isinstance(rows, pl.BlockSpec):
            return rows
        if rows is None:
            return pl.BlockSpec(shape, lambda i: (0,) * len(shape))
        return pl.BlockSpec((rows,) + tuple(shape[1:]), lambda i: (i,) + (0,) * (len(shape) - 1))

    size = sum(math.prod(a.shape) * a.dtype.itemsize for a, _ in ins + outs)
    return pl.pallas_call(
        kernel,
        grid=(steps,),
        in_specs=[spec(a.shape, rows) for a, rows in ins],
        out_specs=[spec(a.shape, rows) for a, rows in outs],
        out_shape=[a for a, _ in outs],
        scratch_shapes=list(scratch),
        compiler_params=pltpu.CompilerParams(vmem_limit_bytes=VMEM),
        cost_estimate=pl.CostEstimate(
            flops=flops >> SHRINK, bytes_accessed=size >> SHRINK, transcendentals=0
        ),
        input_output_aliases=aliases or {},
        name=name,
    )(*[a for a, _ in ins])


def kept(dims, dtype):
    return pltpu.HBM(dims, dtype) if FAR else jax.ShapeDtypeStruct(dims, dtype)


def shape(dims, dtype):
    return jax.ShapeDtypeStruct(dims, dtype)


def conv_a_kernel(edge_ref, x_ref, w_ref, pre_ref, sums_ref):
    step = pl.program_id(0)
    rows = x_ref.shape[0]
    per = rows // CELLS
    steps = FRAMES // per
    for one in range(per):
        frame = step * per + one
        values = x_ref[one * CELLS : (one + 1) * CELLS, :]

        here = pl.ds(pl.multiple_of(frame * CELLS, CELLS), CELLS)
        after = pl.ds(pl.multiple_of((frame + 1) * CELLS, CELLS), CELLS)
        before = pl.ds(pl.multiple_of(jnp.maximum(frame - 1, 0) * CELLS, CELLS), CELLS)
        middle = dot(values, w_ref[1])

        @pl.when(frame == 0)
        def _():
            pre_ref[here, :] = middle

        @pl.when(frame > 0)
        def _():
            pre_ref[here, :] += middle
            pre_ref[before, :] += dot(values, w_ref[2])

        @pl.when(frame < FRAMES - 1)
        def _():
            pre_ref[after, :] = dot(values, w_ref[0])

    @pl.when(step == steps - 1)
    def _():
        edge = edge_ref[0]
        inside = inside_of(edge, CELLS)

        def body(frame, sums):
            v = pre_ref[pl.ds(pl.multiple_of(frame * CELLS, CELLS), CELLS), :]
            m = v * inside
            return sums[0] + total(m), sums[1] + total(m * v)

        zero = jnp.zeros((1, pre_ref.shape[1]), full)
        first, second = lax.fori_loop(0, FRAMES, body, (zero, zero))
        sums_ref[0:1, :] = first
        sums_ref[1:2, :] = second
        sums_ref[2:3, :] = jnp.full(zero.shape, (FRAMES * edge * edge).astype(full))


def shift_columns(values, step):
    if step == 0:
        return values
    rows = values.shape[0]
    column = lax.broadcasted_iota(jnp.int32, (rows, 1), 0) & (GRID - 1)
    edge = GRID - 1 if step == 1 else 0
    moved = pltpu.roll(values, (-step) % rows, 0)
    return jnp.where(column == edge, 0.0, moved)


def spread_taps(values, wide_ref):
    wide_ref[:GRID, :] = jnp.zeros((GRID, 3 * MID), low)
    wide_ref[GRID + CELLS :, :] = jnp.zeros((GRID, 3 * MID), low)
    for step in (-1, 0, 1):
        wide_ref[GRID : GRID + CELLS, (step + 1) * MID : (step + 2) * MID] = shift_columns(
            values, step
        ).astype(low)


def conv_b_kernel(edge_ref, count_ref, pre_ref, sums_a_ref, params_ref, w_ref, hidden_ref, out_ref, sums_ref, wide_ref):
    count = count_ref[2:3, 0:1]
    inside = inside_of(edge_ref[0], CELLS)
    scale, offset, _, _ = norm_terms(sums_a_ref, params_ref, count)
    first = jnp.zeros((1, MID), full)
    second = first
    for one in range(pre_ref.shape[0] // CELLS):
        part = slice(one * CELLS, (one + 1) * CELLS)
        hidden = gelu(pre_ref[part, :] * scale + offset) * inside
        hidden_ref[part, :] = hidden.astype(low)
        wide = wide_ref.at[one]
        spread_taps(hidden, wide)
        values = dot(wide[0:CELLS, :], w_ref[0])
        values += dot(wide[GRID : GRID + CELLS, :], w_ref[1])
        values += dot(wide[2 * GRID : 2 * GRID + CELLS, :], w_ref[2])
        out_ref[part, :] = values
        m = values * inside
        first += total(m)
        second += total(m * values)
    add_to(sums_ref, 0, first)
    add_to(sums_ref, 1, second)


def conv_c_kernel(edge_ref, count_ref, pre_ref, sums_b_ref, params_ref, w_ref, hidden_ref, sums_ref):
    count = count_ref[2:3, 0:1]
    inside = inside_of(edge_ref[0], pre_ref.shape[0])
    scale, offset, _, _ = norm_terms(sums_b_ref, params_ref, count)
    hidden = (gelu(pre_ref[...] * scale + offset) * inside).astype(low)
    hidden_ref[...] = hidden
    values = dot(hidden, w_ref[...])
    add_to(sums_ref, 0, total(values))
    add_to(sums_ref, 1, total(values * values))


def pool_matrix(rows, columns, weight):
    pooled = lax.broadcasted_iota(jnp.int32, (rows, columns), 0) & (HALF - 1)
    cell = lax.broadcasted_iota(jnp.int32, (rows, columns), 1)
    same = ((cell >> 5) == (pooled >> 3)) & (((cell >> 1) & 7) == (pooled & 7))
    return jnp.where(same, weight, 0.0).astype(low)


def spread_matrix(rows, columns, weight):
    cell = lax.broadcasted_iota(jnp.int32, (rows, columns), 0)
    pooled = lax.broadcasted_iota(jnp.int32, (rows, columns), 1) & (HALF - 1)
    same = ((cell >> 5) == (pooled >> 3)) & (((cell >> 1) & 7) == (pooled & 7))
    return jnp.where(same, weight, 0.0).astype(low)


def embed_kernel(edge_ref, count_ref, hidden_ref, x_ref, sums_c_ref, params_ref, w_c_ref, w_ref, mixed_ref, pooled_ref, query_ref, key_ref, value_ref):
    count = count_ref[2:3, 0:1]
    inside = inside_of(edge_ref[0], CELLS)
    scale, offset, _, _ = norm_terms(sums_c_ref, params_ref, count)
    pool = pool_matrix(HALF, CELLS, 0.25)
    for one in range(hidden_ref.shape[0] // CELLS):
        part = slice(one * CELLS, (one + 1) * CELLS)
        piece = slice(one * HALF, (one + 1) * HALF)
        joined = dot(hidden_ref[part, :], w_c_ref[...]) * scale + offset + x_ref[part, :].astype(full)
        mixed = (gelu(joined) * inside).astype(low)
        mixed_ref[part, :] = mixed
        query_ref[part, :] = dot(mixed, w_ref[0]).astype(low)
        pooled = dot(pool, mixed).astype(low)
        pooled_ref[piece, :] = pooled
        key_ref[piece, :] = dot(pooled, w_ref[1]).astype(low)
        value_ref[piece, :] = dot(pooled, w_ref[2]).astype(low)


def attend_kernel(edge_ref, query_ref, key_ref, value_ref, w_out_ref, cot_ref, probs_ref, attended_ref, pre_ref, sums_ref):
    edge = edge_ref[0]
    rows = query_ref.shape[0]
    inside = inside_of(edge, rows)
    keys = key_ref.shape[0]
    spot = lax.broadcasted_iota(jnp.int32, (1, keys), 1)
    keyed = (((spot >> 3) & 7) * 2 < edge) & ((spot & 7) * 2 < edge)
    scores = dot_cols(query_ref[...], key_ref[...]) * (query_ref.shape[1] ** -0.5)
    scores = jnp.where(keyed, scores, masked_score)
    weights = jnp.exp(scores - jnp.max(scores, axis=1, keepdims=True))
    probs = weights * (inside / jnp.sum(weights, axis=1, keepdims=True))
    probs = probs.astype(low)
    probs_ref[...] = probs
    attended = dot(probs, value_ref[...]).astype(low)
    attended_ref[...] = attended
    values = dot(attended, w_out_ref[...])
    pre_ref[...] = values.astype(low)
    upstream = cot_ref[...].astype(full) * inside
    add_to(sums_ref, 0, total(values))
    add_to(sums_ref, 1, total(values * values))
    add_to(sums_ref, 2, total(upstream))
    add_to(sums_ref, 3, total(upstream * values))


def attend_back_kernel(edge_ref, count_ref, pre_ref, mixed_ref, cot_ref, probs_ref, query_ref, key_ref, value_ref, w_out_ref, w_ref, sums_ref, params_ref, out_ref, back_ref, grad_query_ref, grad_key_ref, grad_value_ref, grad_pooled_ref, key_total, value_total):
    step = pl.program_id(0)
    count = count_ref[2:3, 0:1]
    inside = inside_of(edge_ref[0], pre_ref.shape[0])
    scale, offset, root, root_offset = norm_terms(sums_ref, params_ref, count)
    shift_grad = sums_ref[2:3]
    gain_grad = sums_ref[3:4] * root + shift_grad * root_offset
    slope, shift = back_terms(shift_grad, gain_grad, scale, root, root_offset, count)
    pre = pre_ref[...].astype(full)
    out_ref[...] = ((pre * scale + offset + mixed_ref[...].astype(full)) * inside).astype(low)
    back = ((cot_ref[...].astype(full) * scale + pre * slope + shift) * inside).astype(low)
    back_ref[...] = back
    grad_attended = dot_cols(back, w_out_ref[...]).astype(low)
    grad_probs = dot_cols(grad_attended, value_ref[...])
    probs_low = probs_ref[...]
    probs = probs_low.astype(full)
    both = probs * grad_probs
    grad_dots = (
        (both - probs * jnp.sum(both, axis=1, keepdims=True)) * (query_ref.shape[1] ** -0.5)
    ).astype(low)
    grad_query_ref[...] = dot(grad_dots, key_ref[...]).astype(low)
    key_part = dot_rows(grad_dots, query_ref[...])
    value_part = dot_rows(probs_low, grad_attended)

    @pl.when(step == 0)
    def _():
        key_total[...] = key_part
        value_total[...] = value_part

    @pl.when(step != 0)
    def _():
        key_total[...] += key_part
        value_total[...] += value_part

    @pl.when(step == pl.num_programs(0) - 1)
    def _():
        grad_key = key_total[...].astype(low)
        grad_value = value_total[...].astype(low)
        grad_key_ref[...] = grad_key
        grad_value_ref[...] = grad_value
        pooled = dot_cols(grad_key, w_ref[1]) + dot_cols(grad_value, w_ref[2])
        upper = pooled.astype(low)
        lower = (pooled - upper.astype(full)).astype(low)
        for frame in range(FRAMES):
            piece = slice(frame * HALF, (frame + 1) * HALF)
            grad_pooled_ref[2 * frame * HALF : (2 * frame + 1) * HALF, :] = upper[piece, :]
            grad_pooled_ref[(2 * frame + 1) * HALF : (2 * frame + 2) * HALF, :] = lower[piece, :]


def local_grads_kernel(mixed_ref, grad_query_ref, pooled_ref, grad_key_ref, grad_value_ref, attended_ref, back_ref, out_ref):
    step = pl.program_id(0)
    rows = out_ref.shape[2]

    def put(grads):
        for shard in range(grads.shape[0] // rows):
            out_ref[shard % 2, shard // 2] = grads[shard * rows : (shard + 1) * rows, :]

    @pl.when(step < 2)
    def _():
        put(dot_rows(mixed_ref[...], grad_query_ref[...]).astype(low))

    @pl.when((step >= 2) & (step < 4))
    def _():
        put(dot_rows(pooled_ref[...], grad_key_ref[...]).astype(low))

    @pl.when((step >= 4) & (step < 6))
    def _():
        put(dot_rows(pooled_ref[...], grad_value_ref[...]).astype(low))

    @pl.when(step >= 6)
    def _():
        grads = dot_rows(attended_ref[...], back_ref[...]).astype(low)
        half = rows // 2
        for shard in range(grads.shape[0] // half):
            part = grads[shard * half : (shard + 1) * half, :]
            out_ref[shard % 2, shard // 2, :half, :] = part[:, :INNER]
            out_ref[shard % 2, shard // 2, half:, :] = part[:, INNER:]


def joined_back_kernel(edge_ref, count_ref, hidden_ref, x_ref, cot_ref, grad_query_ref, grad_pooled_ref, w_c_ref, w_theta_ref, sums_c_ref, params_ref, grad_ref, sums_ref):
    count = count_ref[2:3, 0:1]
    inside = inside_of(edge_ref[0], CELLS)
    scale, offset, root, root_offset = norm_terms(sums_c_ref, params_ref, count)
    spread = spread_matrix(CELLS, 2 * HALF, 0.25)
    first = jnp.zeros((1, x_ref.shape[1]), full)
    second = first
    for one in range(hidden_ref.shape[0] // CELLS):
        part = slice(one * CELLS, (one + 1) * CELLS)
        pre = dot(hidden_ref[part, :], w_c_ref[...])
        joined = pre * scale + offset + x_ref[part, :].astype(full)
        grad = cot_ref[part, :].astype(full) + dot_cols(grad_query_ref[part, :], w_theta_ref[0])
        grad += dot(spread, grad_pooled_ref[2 * one * HALF : 2 * (one + 1) * HALF, :])
        grad = grad * inside * gelu_slope(joined)
        grad_ref[part, :] = grad.astype(low)
        first += total(grad)
        second += total(grad * (pre * root + root_offset))
    add_to(sums_ref, 0, first)
    add_to(sums_ref, 1, second)


def expand_back_kernel(edge_ref, count_ref, grad_ref, hidden_ref, pre_b_ref, w_c_ref, sums_c_ref, params_c_ref, back_sums_ref, sums_b_ref, params_b_ref, back_ref, out_ref, sums_ref):
    count = count_ref[2:3, 0:1]
    inside = inside_of(edge_ref[0], grad_ref.shape[0])
    scale, _, root, root_offset = norm_terms(sums_c_ref, params_c_ref, count)
    slope, shift = back_terms(back_sums_ref[0:1], back_sums_ref[1:2], scale, root, root_offset, count)
    pre = dot(hidden_ref[...], w_c_ref[...])
    back = ((grad_ref[...].astype(full) * scale + pre * slope + shift) * inside).astype(low)
    back_ref[...] = back
    scale, offset, root, root_offset = norm_terms(sums_b_ref, params_b_ref, count)
    pre = pre_b_ref[...]
    grad = dot_cols(back, w_c_ref[...]) * inside * gelu_slope(pre * scale + offset)
    out_ref[...] = grad
    add_to(sums_ref, 0, total(grad))
    add_to(sums_ref, 1, total(grad * (pre * root + root_offset)))


def conv_b_back_kernel(edge_ref, count_ref, grad_ref, pre_b_ref, sums_b_ref, params_b_ref, back_sums_ref, pre_a_ref, sums_a_ref, params_a_ref, w_ref, back_ref, out_ref, sums_ref, wide_ref):
    count = count_ref[2:3, 0:1]
    inside = inside_of(edge_ref[0], CELLS)
    scale, _, root, root_offset = norm_terms(sums_b_ref, params_b_ref, count)
    slope, shift = back_terms(back_sums_ref[0:1], back_sums_ref[1:2], scale, root, root_offset, count)
    scale_a, offset_a, root_a, root_offset_a = norm_terms(sums_a_ref, params_a_ref, count)
    first = jnp.zeros((1, MID), full)
    second = first
    for one in range(grad_ref.shape[0] // CELLS):
        part = slice(one * CELLS, (one + 1) * CELLS)
        back = (grad_ref[part, :] * scale + pre_b_ref[part, :] * slope + shift) * inside
        back_ref[part, :] = back.astype(low)
        wide = wide_ref.at[one]
        spread_taps(back, wide)
        grad = jnp.zeros((CELLS, MID), full)
        for row_step in (-1, 0, 1):
            for col_step in (-1, 0, 1):
                tap = 3 * (row_step + 1) + col_step + 1
                at = GRID - GRID * row_step
                place = 1 - col_step
                grad += dot_cols(
                    wide[at : at + CELLS, place * MID : (place + 1) * MID], w_ref[tap]
                )
        pre = pre_a_ref[part, :]
        grad = grad * inside * gelu_slope(pre * scale_a + offset_a)
        out_ref[part, :] = grad
        first += total(grad)
        second += total(grad * (pre * root_a + root_offset_a))
    add_to(sums_ref, 0, first)
    add_to(sums_ref, 1, second)


def tap_grads_kernel(hidden_ref, back_ref, expand_ref, near_ref, far_ref, wide_ref, tall_ref):
    near = near_ref.shape[0]
    step = pl.program_id(0)

    @pl.when(step == 0)
    def _():
        rows = FRAMES * CELLS
        for frame in range(FRAMES):
            part = slice(frame * CELLS, (frame + 1) * CELLS)
            values = hidden_ref[part, :].astype(full)
            for col_step in (-1, 0, 1):
                moved = shift_columns(values, col_step).astype(low)
                wide_ref[col_step + 1, :, part] = moved.T
            back = back_ref[part, :]
            zero = jnp.zeros((GRID, MID), low)
            start = frame * CELLS
            tall_ref[0, start : start + CELLS - GRID, :] = back[GRID:]
            tall_ref[0, start + CELLS - GRID : start + CELLS, :] = zero
            tall_ref[1, part, :] = back
            tall_ref[2, start : start + GRID, :] = zero
            tall_ref[2, start + GRID : start + CELLS, :] = back[: CELLS - GRID]

    for tap in range(9):

        @pl.when(step == tap)
        def _():
            grads = dot(wide_ref[tap % 3], tall_ref[tap // 3]).astype(low)
            start = tap * MID - near
            if start < 0:
                near_ref[...] = grads[:near]
                far_ref[: MID - near, :] = grads[near:]
            else:
                far_ref[start : start + MID, :] = grads

    @pl.when(step == pl.num_programs(0) - 1)
    def _():
        far_ref[9 * MID - near :, :] = expand_ref[...]


def frame_grads_kernel(edge_ref, count_ref, grad_ref, pre_ref, sums_a_ref, params_ref, back_sums_ref, turned_ref, rest_ref, back_ref, out_ref):
    step = pl.program_id(0)
    rows = grad_ref.shape[0]

    @pl.when(step == 0)
    def _():
        count = count_ref[2:3, 0:1]
        inside = inside_of(edge_ref[0], CELLS)
        scale, _, root, root_offset = norm_terms(sums_a_ref, params_ref, count)
        slope, shift = back_terms(
            back_sums_ref[0:1], back_sums_ref[1:2], scale, root, root_offset, count
        )
        back_ref[:CELLS, :] = jnp.zeros((CELLS, MID), low)
        back_ref[rows + CELLS :, :] = jnp.zeros((CELLS, MID), low)
        for frame in range(FRAMES):
            part = slice(frame * CELLS, (frame + 1) * CELLS)
            back = (grad_ref[part, :] * scale + pre_ref[part, :] * slope + shift) * inside
            back_ref[(frame + 1) * CELLS : (frame + 2) * CELLS, :] = back.astype(low)

    blocks = turned_ref.shape[0] // MID
    offset = step // blocks
    across = pl.ds(pl.multiple_of((step - offset * blocks) * MID, MID), MID)
    start = pl.multiple_of((2 - offset) * CELLS, CELLS)
    place = pl.ds(pl.multiple_of(step * MID, MID), MID)
    out_ref[place, :] = dot(turned_ref[across, :], back_ref[pl.ds(start, rows), :]).astype(low)

    @pl.when(step == pl.num_programs(0) - 1)
    def _():
        out_ref[pl.num_programs(0) * MID :, :] = rest_ref[...]


def input_back_kernel(back_ref, grad_ref, w_ref, out_ref):
    step = pl.program_id(0)
    rows = grad_ref.shape[0]
    grad = grad_ref[...].astype(full)
    for offset in range(3):
        start = pl.multiple_of(step * rows + (2 - offset) * CELLS, CELLS)
        grad += dot_cols(back_ref[pl.ds(start, rows), :], w_ref[offset])
    out_ref[...] = grad.astype(low)


def on_device(
    clips_in,
    crop_edges,
    cotangent,
    bottle_weights,
    bottle_momentum,
    local_weights,
    local_momentum,
    norm_params,
    norm_momentum,
):
    clip_count, position_count, channels = clips_in.shape
    assert clip_count == 1 and position_count == FRAMES * CELLS
    rows = position_count
    keys = FRAMES * HALF
    x = clips_in.reshape(rows, channels)
    cot = cotangent.reshape(rows, channels)
    edge = (crop_edges, "smem")

    bits = bit_count()
    top = bits - 1
    inner = list(range(top - 1, -1, -1))
    mine = bottle_weights.astype(low).reshape(-1, MID)
    other = swap(mine, 1 << top)
    high = device_bit(top) == 1
    near = Gather(jnp.where(high, other, mine), inner)
    far = Gather(jnp.where(high, mine, other), inner)
    local_low = local_weights.astype(low).reshape(-1, INNER)
    turned = x.T
    for number in range(len(inner)):
        near.send()
        if number > 0:
            far.values = after(far.values, near.values)
            far.send()
        if 0 < number < len(inner) - 1:
            near.got = far.beside(near.got)
        if number == len(inner) - 2:
            near.got, turned, local_low = lax.optimization_barrier((near.got, turned, local_low))
        near.take()
        if 0 < number < len(inner) - 1:
            far.take()
    near_full = near.result()
    local_low = after(local_low, near_full)
    local_full = lax.all_gather(local_low, AXES, axis=0, tiled=True)
    first = 3 * channels
    weight_a = near_full[:first].reshape(3, channels, MID)
    w_in = local_full[: 3 * channels].reshape(3, channels, INNER)
    w_out = local_full[3 * channels :].reshape(INNER, channels)
    params_a = norm_params[: 2 * MID].reshape(2, MID)
    params_b = norm_params[2 * MID : 4 * MID].reshape(2, MID)
    params_c = norm_params[4 * MID : 4 * MID + 2 * channels].reshape(2, channels)
    params_n = norm_params[4 * MID + 2 * channels :].reshape(2, channels)

    step = STEP * CELLS
    steps = rows // step
    matmul = 2 * rows * MID * channels
    pre_a, part = call(
        conv_a_kernel,
        steps,
        [edge, (x, step), (weight_a, None)],
        [(shape((rows, MID), full), None), (shape((3, MID), full), None)],
        flops=3 * matmul,
        name="conv_a",
    )
    part = far.beside(part)
    far.take()
    far.send()
    sums_a = far.beside(sum_small(part) if WHOLE & 1 else sum_devices(part))
    far.take()
    far_full = far.result()
    rest = first + 9 * MID - near_full.shape[0]
    weight_b = jnp.concatenate([near_full[first:], far_full[:rest]])
    weight_c = far_full[rest:].reshape(MID, channels)
    count = (sums_a, None)
    hidden_a, pre_b, part = call(
        conv_b_kernel,
        steps,
        [edge, count, (pre_a, step), (sums_a, None), (params_a, None), (weight_b.reshape(3, 3 * MID, MID), None)],
        [(kept((rows, MID), low), step), (shape((rows, MID), full), step), (shape((2, MID), full), None)],
        [pltpu.VMEM((step // CELLS, CELLS + 2 * GRID, 3 * MID), low)],
        flops=9 * matmul // 4,
        name="conv_b",
    )
    sums_b = sum_small(part) if WHOLE & 1 else sum_devices(part)
    hidden_b, part = call(
        conv_c_kernel,
        steps,
        [edge, count, (pre_b, step), (sums_b, None), (params_b, None), (weight_c, None)],
        [(shape((rows, MID), low), step), (shape((2, channels), full), None)],
        flops=matmul,
        name="conv_c",
    )
    sums_c = sum_pairs(part) if PAIRS & 1 else sum_devices(part)
    mixed, pooled, query, key_rows, value_rows = call(
        embed_kernel,
        steps,
        [edge, count, (hidden_b, step), (x, step), (sums_c, None), (params_c, None), (weight_c, None), (w_in, None)],
        [
            (kept((rows, channels), low), step),
            (kept((keys, channels), low), step // 4),
            (shape((rows, INNER), low), step),
            (shape((keys, INNER), low), step // 4),
            (shape((keys, INNER), low), step // 4),
        ],
        flops=4 * matmul,
        name="embed",
    )
    probs, attended, pre_w, part = call(
        attend_kernel,
        steps,
        [edge, (query, step), (key_rows, None), (value_rows, None), (w_out, None), (cot, step)],
        [
            (kept((rows, keys), low), step),
            (kept((rows, INNER), low), step),
            (kept((rows, channels), low), step),
            (shape((4, channels), full), None),
        ],
        flops=4 * matmul,
        name="attend",
    )
    sums_n = sum_devices(part)
    clips_out, back_w, grad_query, grad_key, grad_value, grad_pooled = call(
        attend_back_kernel,
        steps,
        [
            edge,
            count,
            (pre_w, step),
            (mixed, step),
            (cot, step),
            (probs, step),
            (query, step),
            (key_rows, None),
            (value_rows, None),
            (w_out, None),
            (w_in, None),
            (sums_n, None),
            (params_n, None),
        ],
        [
            (shape((rows, channels), low), step),
            (shape((rows, channels), low), step),
            (shape((rows, INNER), low), step),
            (shape((keys, INNER), low), None),
            (shape((keys, INNER), low), None),
            (shape((2 * keys, channels), low), None),
        ],
        [pltpu.VMEM((keys, INNER), full), pltpu.VMEM((keys, INNER), full)],
        flops=7 * matmul,
        name="attend_back",
    )
    shard_rows = local_low.shape[0]
    pairs = device_count() // 2
    if shard_rows % 32 == 0:

        def columns(width, at):
            return pl.BlockSpec((rows, width), lambda i: (0, at(i)))

        (local_grads,) = call(
            local_grads_kernel,
            8,
            [
                (mixed, columns(2 * MID, lambda i: jnp.minimum(i, 1))),
                (grad_query, None),
                (pooled, pl.BlockSpec((keys, 2 * MID), lambda i: (0, i & 1))),
                (grad_key, None),
                (grad_value, None),
                (attended, columns(MID, lambda i: jnp.maximum(i - 6, 0))),
                (back_w, None),
            ],
            [
                (
                    shape((2, pairs, shard_rows, INNER), low),
                    pl.BlockSpec((2, pairs // 8, shard_rows, INNER), lambda i: (0, i, 0, 0)),
                )
            ],
            flops=5 * matmul,
            name="local_grads",
        )
    else:
        grad_out = dot_rows(attended, back_w).astype(low)
        grad_out = grad_out.reshape(-1, shard_rows // 2, 2, INNER).transpose(0, 2, 1, 3)
        local_grads = jnp.concatenate(
            [
                dot_rows(mixed, grad_query).astype(low),
                dot_rows(pooled, grad_key).astype(low),
                dot_rows(pooled, grad_value).astype(low),
                grad_out.reshape(-1, INNER),
            ]
        )
        local_grads = local_grads.reshape(pairs, 2, shard_rows, INNER).transpose(1, 0, 2, 3)
    spans = list(range(top, 0, -1))
    local = Scatter(local_grads, [0], [0] + spans)
    local.send()
    grad_query = local.beside(grad_query)
    local.take()
    local = Halves(local.values, 1, top, spans)
    local.send()
    grad_joined, part = call(
        joined_back_kernel,
        steps,
        [
            edge,
            count,
            (hidden_b, step),
            (x, step),
            (cot, step),
            (grad_query, step),
            (grad_pooled, step // 2),
            (weight_c, None),
            (w_in, None),
            (sums_c, None),
            (params_c, None),
        ],
        [(shape((rows, channels), low), step), (shape((2, channels), full), None)],
        flops=4 * matmul,
        name="joined_back",
    )
    part = local.beside(part)
    local.take()
    local.send()
    back_sums_c = local.beside(sum_pairs(part) if PAIRS & 2 else sum_devices(part))
    local.take()
    local = local.whole(range(2, top))
    local.send()
    back_c, grad_b, part = call(
        expand_back_kernel,
        steps,
        [
            edge,
            count,
            (grad_joined, step),
            (hidden_b, step),
            (pre_b, step),
            (weight_c, None),
            (sums_c, None),
            (params_c, None),
            (back_sums_c, None),
            (sums_b, None),
            (params_b, None),
        ],
        [
            (shape((rows, channels), low), step),
            (shape((rows, MID), full), step),
            (shape((2, MID), full), None),
        ],
        flops=2 * matmul,
        name="expand_back",
    )
    back_sums_b = local.beside(sum_small(part) if WHOLE & 2 else sum_devices(part))
    local.take()
    local.send()
    grad_weight_c = dot_rows(hidden_b, back_c).astype(low)
    back_b, grad_a, part = call(
        conv_b_back_kernel,
        steps,
        [
            edge,
            count,
            (grad_b, step),
            (pre_b, step),
            (sums_b, None),
            (params_b, None),
            (back_sums_b, None),
            (pre_a, step),
            (sums_a, None),
            (params_a, None),
            (weight_b.reshape(9, MID, MID), None),
        ],
        [
            (shape((rows, MID), low), step),
            (shape((rows, MID), full), step),
            (shape((2, MID), full), None),
        ],
        [pltpu.VMEM((step // CELLS, CELLS + 2 * GRID, 3 * MID), low)],
        flops=9 * matmul // 4,
        name="conv_b_back",
    )
    half = near_full.shape[0]
    near_grads, far_grads = call(
        tap_grads_kernel,
        10,
        [(hidden_a, None), (back_b, None), (grad_weight_c.reshape(-1, MID), None)],
        [(shape((half - first, MID), low), None), (shape((half, MID), low), None)],
        [pltpu.VMEM((3, MID, rows), low), pltpu.VMEM((3, rows, MID), low)],
        flops=9 * matmul // 4,
        name="tap_grads",
    )
    part = local.beside(part)
    local.take()
    while local.order:
        local.send()
        local.take()
    spans = list(range(top - 1, 0, -1))
    far = Scatter(far_grads, [0], spans + [0])
    far.send()
    if WHOLE & 2:
        back_sums_a = far.beside(sum_small(part))
    else:
        back_sums_a = sum_devices(part, far.beside)
    far.take()
    far = Halves(far.values, 1, 2, spans)
    far.send()
    padded, near_grads = call(
        frame_grads_kernel,
        first // MID,
        [
            edge,
            count,
            (grad_a, None),
            (pre_a, None),
            (sums_a, None),
            (params_a, None),
            (back_sums_a, None),
            (turned, None),
            (near_grads, None),
        ],
        [(shape((rows + 2 * CELLS, MID), low), None), (shape((half, MID), low), None)],
        flops=3 * matmul,
        name="frame_grads",
    )
    near_grads = far.beside(near_grads)
    near = Scatter(near_grads, [0], spans + [0])
    near.send()
    far.take()
    far.send()
    padded = near.beside(padded)
    near.take()
    near = Halves(near.values, 1, 2, spans)
    near.send()
    (clips_grad,) = call(
        input_back_kernel,
        steps,
        [(padded, None), (grad_joined, step), (weight_a, None)],
        [(shape((rows, channels), low), step)],
        flops=3 * matmul,
        name="input_back",
    )
    clips_grad = near.beside(far.beside(clips_grad))
    near.take()
    near.send()
    far.take()
    far = far.whole(range(3, top))
    while far.order:
        far.send()
        far.take()
    near.take()
    near = near.whole(range(3, top))
    while near.order:
        near.send()
        near.take()
    near_sum, far_sum = near.values, far.values
    got = swap(jnp.where(high, near_sum, far_sum).astype(low), 1 << top)
    bottle_shard = (jnp.where(high, far_sum, near_sum) + got.astype(full)).reshape(-1)
    local_sum = local.values.astype(full)
    halves = local_sum.reshape(2, -1, INNER)
    joint = jnp.concatenate([halves[0], halves[1]], axis=1).reshape(-1)
    in_out = lax.axis_index(AXES) * shard_rows >= 3 * channels
    local_shard = jnp.where(in_out, joint, local_sum.reshape(-1))
    clips_total = clip_count * device_count()
    mean_n, root_n = moments(sums_n, sums_a[2, 0])
    gain_n_grad = root_n[0] * (sums_n[3] - mean_n[0] * sums_n[2])
    norm_grad = jnp.concatenate(
        [
            back_sums_a[1],
            back_sums_a[0],
            back_sums_b[1],
            back_sums_b[0],
            back_sums_c[1],
            back_sums_c[0],
            gain_n_grad,
            sums_n[2],
        ]
    )
    bottle_velocity = (
        momentum_rate * bottle_momentum + bottle_shard / clips_total + decay_rate * bottle_weights
    )
    local_velocity = (
        momentum_rate * local_momentum + local_shard / clips_total + decay_rate * local_weights
    )
    norm_velocity = momentum_rate * norm_momentum + norm_grad / clips_total
    return (
        clips_out.reshape(clips_in.shape),
        clips_grad.reshape(clips_in.shape),
        bottle_weights - learning_rate * bottle_velocity,
        bottle_velocity,
        local_weights - learning_rate * local_velocity,
        local_velocity,
        norm_params - learning_rate * norm_velocity,
        norm_velocity,
    )


def solution(mesh):
    devices = mesh.devices.reshape(mesh.shape["dp"], mesh.shape["fsdp"] // 2, 2)
    split = P(AXES)
    return jax.shard_map(
        on_device,
        mesh=Mesh(devices, AXES),
        in_specs=(split,) * 7 + (P(),) * 2,
        out_specs=(split,) * 6 + (P(),) * 2,
        check_vma=False,
    )
```

```python
import math

import jax
import jax.numpy as jnp
from jax import lax
from jax.experimental import pallas as pl
from jax.experimental.pallas import tpu as pltpu
from jax.sharding import Mesh
from jax.sharding import PartitionSpec as P

MID = 256
INNER = 512
FRAMES = 8
GRID = 16
CELLS = GRID * GRID
HALF = CELLS // 4

epsilon = 1e-05
learning_rate = 0.01
momentum_rate = 0.9
decay_rate = 0.0001
masked_score = -1e30
curve = 0.7978845608028654
cubic = 0.044715

VMEM = 32 * 1024 * 1024
STEP = 2
SHRINK = 10
FAR = 1
BIG = 768
NAMES = ("conv_a", "conv_b", "conv_c", "embed", "attend", "attend_back", "local_grads", "joined_back", "expand_back", "conv_b_back", "tap_grads", "frame_grads", "input_back")
WHOLE = 3
PAIRS = 3
low = jnp.bfloat16
full = jnp.float32


RINGS = ("dp", "ring")
AXES = RINGS + ("core",)


def device_count():
    return lax.axis_size(AXES)


def device_bit(bit):
    return (lax.axis_index(AXES) >> bit) & 1


def bit_count():
    count = device_count()
    bits = count.bit_length() - 1
    assert count == 1 << bits
    return bits


def swap(values, mask):
    count = device_count()
    return lax.ppermute(values, AXES, [(i, i ^ mask) for i in range(count)])


def sum_devices(values, between=lambda values: values):
    bits = bit_count()
    groups = [[0]]
    low, high = 1, bits - 1
    while low <= high:
        groups.append([low, high] if low < high else [low])
        low, high = low + 1, high - 1
    for number, group in enumerate(groups):
        if number == len(groups) - 1:
            values = between(values)
        if len(group) == 1:
            values = values + swap(values, 1 << group[0])
        else:
            one, two = 1 << group[0], 1 << group[1]
            near, far, both = swap(values, one), swap(values, two), swap(values, one | two)
            values = (values + near) + (far + both)
    return values


def after(values, *others):
    return lax.optimization_barrier((values,) + others)[0]


def sum_small(values, axes=AXES):
    copies = jnp.broadcast_to(values[None], (lax.axis_size(axes),) + values.shape)
    return jnp.sum(lax.all_to_all(copies, axes, 0, 0), axis=0)


def sum_pairs(values):
    return sum_small(values + swap(values, 1), RINGS)


class Moving:
    def beside(self, other):
        self.got, other = lax.optimization_barrier((self.got, other))
        return other


class Gather(Moving):
    def __init__(self, rows, order):
        self.values, self.order, self.present = rows, list(order[1:]), [order[0]]
        self.tail = rows.shape[1:]

    def send(self):
        self.bit = self.order.pop(0)
        self.got = swap(self.values, 1 << self.bit)

    def take(self):
        mine = device_bit(self.bit) == 1
        position = sum(1 for have in self.present if have > self.bit)
        self.values = jnp.stack(
            [jnp.where(mine, self.got, self.values), jnp.where(mine, self.values, self.got)],
            axis=position,
        )
        self.present.append(self.bit)

    def result(self):
        return self.values.reshape((-1,) + self.tail[1:])


class Scatter(Moving):
    def __init__(self, values, order, present):
        self.values = values.reshape((2,) * len(present) + (-1, values.shape[-1]))
        self.present = list(present)
        self.order = list(order)

    def send(self):
        bit = self.order.pop(0)
        position = self.present.index(bit)
        upper = lax.index_in_dim(self.values, 1, position, keepdims=False)
        lower = lax.index_in_dim(self.values, 0, position, keepdims=False)
        mine = device_bit(bit) == 1
        self.keep = jnp.where(mine, upper, lower)
        self.got = swap(jnp.where(mine, lower, upper), 1 << bit)
        self.present.remove(bit)

    def take(self):
        self.values = self.keep.astype(full) + self.got.astype(full)
        if self.present:
            self.values = self.values.astype(low)


class Halves:
    def __init__(self, values, one, two, present):
        width = values.shape[-1] // 2
        self.left = Scatter(values[..., :width], [one, two], present)
        self.right = Scatter(values[..., width:], [two, one], present)

    def send(self):
        self.left.send()
        self.right.send()

    def beside(self, other):
        self.left.got, self.right.got, other = lax.optimization_barrier(
            (self.left.got, self.right.got, other)
        )
        return other

    def take(self):
        self.left.take()
        self.right.take()

    def whole(self, order):
        values = jnp.concatenate([self.left.values, self.right.values], axis=-1)
        return Scatter(values, order, self.left.present)


def dot(left, right):
    return jnp.dot(left, right, preferred_element_type=full)


def dot_cols(left, right):
    return lax.dot_general(left, right, (((1,), (1,)), ((), ())), preferred_element_type=full)


def dot_rows(left, right):
    return lax.dot_general(left, right, (((0,), (0,)), ((), ())), preferred_element_type=full)


def gelu(v):
    return 0.5 * v * (1.0 + jnp.tanh(curve * (v + cubic * (v * v * v))))


def gelu_slope(v):
    square = v * v
    bend = jnp.tanh(v * (curve + (curve * cubic) * square))
    half = 0.5 * v
    return 0.5 + 0.5 * bend + half * (1.0 - bend * bend) * (curve + (3.0 * curve * cubic) * square)


def inside_of(edge, rows):
    cell = lax.broadcasted_iota(jnp.int32, (rows, 1), 0) & (CELLS - 1)
    return (((cell >> 4) < edge) & ((cell & 15) < edge)).astype(full)


def total(values):
    return jnp.sum(values, axis=0, keepdims=True)


def moments(sums_ref, count):
    mean = sums_ref[0:1] / count
    return mean, lax.rsqrt(sums_ref[1:2] / count - mean * mean + epsilon)


def norm_terms(sums_ref, params_ref, count):
    mean, root = moments(sums_ref, count)
    scale = root * params_ref[0:1]
    return scale, params_ref[1:2] - mean * scale, root, -mean * root


def back_terms(shift_grad, gain_grad, scale, root, root_offset, count):
    slope = -(scale * gain_grad * root) / count
    offset = -(scale * (shift_grad + gain_grad * root_offset)) / count
    return slope, offset


def add_to(ref, row, value):
    @pl.when(pl.program_id(0) == 0)
    def _():
        ref[row : row + 1, :] = value

    @pl.when(pl.program_id(0) != 0)
    def _():
        ref[row : row + 1, :] += value


def call(kernel, steps, ins, outs, scratch=(), flops=0, name=None, aliases=None):
    def spec(shape, rows):
        if rows == "smem":
            return pl.BlockSpec(memory_space=pltpu.SMEM)
        if isinstance(rows, pl.BlockSpec):
            return rows
        if rows is None:
            return pl.BlockSpec(shape, lambda i: (0,) * len(shape))
        return pl.BlockSpec((rows,) + tuple(shape[1:]), lambda i: (i,) + (0,) * (len(shape) - 1))

    size = sum(math.prod(a.shape) * a.dtype.itemsize for a, _ in ins + outs)
    return pl.pallas_call(
        kernel,
        grid=(steps,),
        in_specs=[spec(a.shape, rows) for a, rows in ins],
        out_specs=[spec(a.shape, rows) for a, rows in outs],
        out_shape=[a for a, _ in outs],
        scratch_shapes=list(scratch),
        compiler_params=pltpu.CompilerParams(vmem_limit_bytes=(62 << 20) if BIG >> NAMES.index(name) & 1 else VMEM),
        cost_estimate=pl.CostEstimate(
            flops=flops >> SHRINK, bytes_accessed=size >> SHRINK, transcendentals=0
        ),
        input_output_aliases=aliases or {},
        name=name,
    )(*[a for a, _ in ins])


def kept(dims, dtype):
    return pltpu.HBM(dims, dtype) if FAR else jax.ShapeDtypeStruct(dims, dtype)


def shape(dims, dtype):
    return jax.ShapeDtypeStruct(dims, dtype)


def conv_a_kernel(edge_ref, x_ref, w_ref, pre_ref, sums_ref):
    step = pl.program_id(0)
    rows = x_ref.shape[0]
    per = rows // CELLS
    steps = FRAMES // per
    for one in range(per):
        frame = step * per + one
        values = x_ref[one * CELLS : (one + 1) * CELLS, :]

        here = pl.ds(pl.multiple_of(frame * CELLS, CELLS), CELLS)
        after = pl.ds(pl.multiple_of((frame + 1) * CELLS, CELLS), CELLS)
        before = pl.ds(pl.multiple_of(jnp.maximum(frame - 1, 0) * CELLS, CELLS), CELLS)
        middle = dot(values, w_ref[1])

        @pl.when(frame == 0)
        def _():
            pre_ref[here, :] = middle

        @pl.when(frame > 0)
        def _():
            pre_ref[here, :] += middle
            pre_ref[before, :] += dot(values, w_ref[2])

        @pl.when(frame < FRAMES - 1)
        def _():
            pre_ref[after, :] = dot(values, w_ref[0])

    @pl.when(step == steps - 1)
    def _():
        edge = edge_ref[0]
        inside = inside_of(edge, CELLS)

        def body(frame, sums):
            v = pre_ref[pl.ds(pl.multiple_of(frame * CELLS, CELLS), CELLS), :]
            m = v * inside
            return sums[0] + total(m), sums[1] + total(m * v)

        zero = jnp.zeros((1, pre_ref.shape[1]), full)
        first, second = lax.fori_loop(0, FRAMES, body, (zero, zero))
        sums_ref[0:1, :] = first
        sums_ref[1:2, :] = second
        sums_ref[2:3, :] = jnp.full(zero.shape, (FRAMES * edge * edge).astype(full))


def shift_columns(values, step):
    if step == 0:
        return values
    rows = values.shape[0]
    column = lax.broadcasted_iota(jnp.int32, (rows, 1), 0) & (GRID - 1)
    edge = GRID - 1 if step == 1 else 0
    moved = pltpu.roll(values, (-step) % rows, 0)
    return jnp.where(column == edge, 0.0, moved)


def spread_taps(values, wide_ref):
    wide_ref[:GRID, :] = jnp.zeros((GRID, 3 * MID), low)
    wide_ref[GRID + CELLS :, :] = jnp.zeros((GRID, 3 * MID), low)
    for step in (-1, 0, 1):
        wide_ref[GRID : GRID + CELLS, (step + 1) * MID : (step + 2) * MID] = shift_columns(
            values, step
        ).astype(low)


def conv_b_kernel(edge_ref, count_ref, pre_ref, sums_a_ref, params_ref, w_ref, hidden_ref, out_ref, sums_ref, wide_ref):
    count = count_ref[2:3, 0:1]
    inside = inside_of(edge_ref[0], CELLS)
    scale, offset, _, _ = norm_terms(sums_a_ref, params_ref, count)
    first = jnp.zeros((1, MID), full)
    second = first
    for one in range(pre_ref.shape[0] // CELLS):
        part = slice(one * CELLS, (one + 1) * CELLS)
        hidden = gelu(pre_ref[part, :] * scale + offset) * inside
        hidden_ref[part, :] = hidden.astype(low)
        wide = wide_ref.at[one]
        spread_taps(hidden, wide)
        values = dot(wide[0:CELLS, :], w_ref[0])
        values += dot(wide[GRID : GRID + CELLS, :], w_ref[1])
        values += dot(wide[2 * GRID : 2 * GRID + CELLS, :], w_ref[2])
        out_ref[part, :] = values
        m = values * inside
        first += total(m)
        second += total(m * values)
    add_to(sums_ref, 0, first)
    add_to(sums_ref, 1, second)


def conv_c_kernel(edge_ref, count_ref, pre_ref, sums_b_ref, params_ref, w_ref, hidden_ref, sums_ref):
    count = count_ref[2:3, 0:1]
    inside = inside_of(edge_ref[0], pre_ref.shape[0])
    scale, offset, _, _ = norm_terms(sums_b_ref, params_ref, count)
    hidden = (gelu(pre_ref[...] * scale + offset) * inside).astype(low)
    hidden_ref[...] = hidden
    values = dot(hidden, w_ref[...])
    add_to(sums_ref, 0, total(values))
    add_to(sums_ref, 1, total(values * values))


def pool_matrix(rows, columns, weight):
    pooled = lax.broadcasted_iota(jnp.int32, (rows, columns), 0) & (HALF - 1)
    cell = lax.broadcasted_iota(jnp.int32, (rows, columns), 1)
    same = ((cell >> 5) == (pooled >> 3)) & (((cell >> 1) & 7) == (pooled & 7))
    return jnp.where(same, weight, 0.0).astype(low)


def spread_matrix(rows, columns, weight):
    cell = lax.broadcasted_iota(jnp.int32, (rows, columns), 0)
    pooled = lax.broadcasted_iota(jnp.int32, (rows, columns), 1) & (HALF - 1)
    same = ((cell >> 5) == (pooled >> 3)) & (((cell >> 1) & 7) == (pooled & 7))
    return jnp.where(same, weight, 0.0).astype(low)


def embed_kernel(edge_ref, count_ref, hidden_ref, x_ref, sums_c_ref, params_ref, w_c_ref, w_ref, mixed_ref, pooled_ref, query_ref, key_ref, value_ref):
    count = count_ref[2:3, 0:1]
    inside = inside_of(edge_ref[0], CELLS)
    scale, offset, _, _ = norm_terms(sums_c_ref, params_ref, count)
    pool = pool_matrix(HALF, CELLS, 0.25)
    for one in range(hidden_ref.shape[0] // CELLS):
        part = slice(one * CELLS, (one + 1) * CELLS)
        piece = slice(one * HALF, (one + 1) * HALF)
        joined = dot(hidden_ref[part, :], w_c_ref[...]) * scale + offset + x_ref[part, :].astype(full)
        mixed = (gelu(joined) * inside).astype(low)
        mixed_ref[part, :] = mixed
        query_ref[part, :] = dot(mixed, w_ref[0]).astype(low)
        pooled = dot(pool, mixed).astype(low)
        pooled_ref[piece, :] = pooled
        key_ref[piece, :] = dot(pooled, w_ref[1]).astype(low)
        value_ref[piece, :] = dot(pooled, w_ref[2]).astype(low)


def attend_kernel(edge_ref, query_ref, key_ref, value_ref, w_out_ref, cot_ref, probs_ref, attended_ref, pre_ref, sums_ref):
    edge = edge_ref[0]
    rows = query_ref.shape[0]
    inside = inside_of(edge, rows)
    keys = key_ref.shape[0]
    spot = lax.broadcasted_iota(jnp.int32, (1, keys), 1)
    keyed = (((spot >> 3) & 7) * 2 < edge) & ((spot & 7) * 2 < edge)
    scores = dot_cols(query_ref[...], key_ref[...]) * (query_ref.shape[1] ** -0.5)
    scores = jnp.where(keyed, scores, masked_score)
    weights = jnp.exp(scores - jnp.max(scores, axis=1, keepdims=True))
    probs = weights * (inside / jnp.sum(weights, axis=1, keepdims=True))
    probs = probs.astype(low)
    probs_ref[...] = probs
    attended = dot(probs, value_ref[...]).astype(low)
    attended_ref[...] = attended
    values = dot(attended, w_out_ref[...])
    pre_ref[...] = values.astype(low)
    upstream = cot_ref[...].astype(full) * inside
    add_to(sums_ref, 0, total(values))
    add_to(sums_ref, 1, total(values * values))
    add_to(sums_ref, 2, total(upstream))
    add_to(sums_ref, 3, total(upstream * values))


def attend_back_kernel(edge_ref, count_ref, pre_ref, mixed_ref, cot_ref, probs_ref, query_ref, key_ref, value_ref, w_out_ref, w_ref, sums_ref, params_ref, out_ref, back_ref, grad_query_ref, grad_key_ref, grad_value_ref, grad_pooled_ref, key_total, value_total):
    step = pl.program_id(0)
    count = count_ref[2:3, 0:1]
    inside = inside_of(edge_ref[0], pre_ref.shape[0])
    scale, offset, root, root_offset = norm_terms(sums_ref, params_ref, count)
    shift_grad = sums_ref[2:3]
    gain_grad = sums_ref[3:4] * root + shift_grad * root_offset
    slope, shift = back_terms(shift_grad, gain_grad, scale, root, root_offset, count)
    pre = pre_ref[...].astype(full)
    out_ref[...] = ((pre * scale + offset + mixed_ref[...].astype(full)) * inside).astype(low)
    back = ((cot_ref[...].astype(full) * scale + pre * slope + shift) * inside).astype(low)
    back_ref[...] = back
    grad_attended = dot_cols(back, w_out_ref[...]).astype(low)
    grad_probs = dot_cols(grad_attended, value_ref[...])
    probs_low = probs_ref[...]
    probs = probs_low.astype(full)
    both = probs * grad_probs
    grad_dots = (
        (both - probs * jnp.sum(both, axis=1, keepdims=True)) * (query_ref.shape[1] ** -0.5)
    ).astype(low)
    grad_query_ref[...] = dot(grad_dots, key_ref[...]).astype(low)
    key_part = dot_rows(grad_dots, query_ref[...])
    value_part = dot_rows(probs_low, grad_attended)

    @pl.when(step == 0)
    def _():
        key_total[...] = key_part
        value_total[...] = value_part

    @pl.when(step != 0)
    def _():
        key_total[...] += key_part
        value_total[...] += value_part

    @pl.when(step == pl.num_programs(0) - 1)
    def _():
        grad_key = key_total[...].astype(low)
        grad_value = value_total[...].astype(low)
        grad_key_ref[...] = grad_key
        grad_value_ref[...] = grad_value
        pooled = dot_cols(grad_key, w_ref[1]) + dot_cols(grad_value, w_ref[2])
        upper = pooled.astype(low)
        lower = (pooled - upper.astype(full)).astype(low)
        for frame in range(FRAMES):
            piece = slice(frame * HALF, (frame + 1) * HALF)
            grad_pooled_ref[2 * frame * HALF : (2 * frame + 1) * HALF, :] = upper[piece, :]
            grad_pooled_ref[(2 * frame + 1) * HALF : (2 * frame + 2) * HALF, :] = lower[piece, :]


def local_grads_kernel(mixed_ref, grad_query_ref, pooled_ref, grad_key_ref, grad_value_ref, attended_ref, back_ref, out_ref):
    step = pl.program_id(0)
    rows = out_ref.shape[2]

    def put(grads):
        for shard in range(grads.shape[0] // rows):
            out_ref[shard % 2, shard // 2] = grads[shard * rows : (shard + 1) * rows, :]

    @pl.when(step < 2)
    def _():
        put(dot_rows(mixed_ref[...], grad_query_ref[...]).astype(low))

    @pl.when((step >= 2) & (step < 4))
    def _():
        put(dot_rows(pooled_ref[...], grad_key_ref[...]).astype(low))

    @pl.when((step >= 4) & (step < 6))
    def _():
        put(dot_rows(pooled_ref[...], grad_value_ref[...]).astype(low))

    @pl.when(step >= 6)
    def _():
        grads = dot_rows(attended_ref[...], back_ref[...]).astype(low)
        half = rows // 2
        for shard in range(grads.shape[0] // half):
            part = grads[shard * half : (shard + 1) * half, :]
            out_ref[shard % 2, shard // 2, :half, :] = part[:, :INNER]
            out_ref[shard % 2, shard // 2, half:, :] = part[:, INNER:]


def joined_back_kernel(edge_ref, count_ref, hidden_ref, x_ref, cot_ref, grad_query_ref, grad_pooled_ref, w_c_ref, w_theta_ref, sums_c_ref, params_ref, grad_ref, sums_ref):
    count = count_ref[2:3, 0:1]
    inside = inside_of(edge_ref[0], CELLS)
    scale, offset, root, root_offset = norm_terms(sums_c_ref, params_ref, count)
    spread = spread_matrix(CELLS, 2 * HALF, 0.25)
    first = jnp.zeros((1, x_ref.shape[1]), full)
    second = first
    for one in range(hidden_ref.shape[0] // CELLS):
        part = slice(one * CELLS, (one + 1) * CELLS)
        pre = dot(hidden_ref[part, :], w_c_ref[...])
        joined = pre * scale + offset + x_ref[part, :].astype(full)
        grad = cot_ref[part, :].astype(full) + dot_cols(grad_query_ref[part, :], w_theta_ref[0])
        grad += dot(spread, grad_pooled_ref[2 * one * HALF : 2 * (one + 1) * HALF, :])
        grad = grad * inside * gelu_slope(joined)
        grad_ref[part, :] = grad.astype(low)
        first += total(grad)
        second += total(grad * (pre * root + root_offset))
    add_to(sums_ref, 0, first)
    add_to(sums_ref, 1, second)


def expand_back_kernel(edge_ref, count_ref, grad_ref, hidden_ref, pre_b_ref, w_c_ref, sums_c_ref, params_c_ref, back_sums_ref, sums_b_ref, params_b_ref, back_ref, out_ref, sums_ref):
    count = count_ref[2:3, 0:1]
    inside = inside_of(edge_ref[0], grad_ref.shape[0])
    scale, _, root, root_offset = norm_terms(sums_c_ref, params_c_ref, count)
    slope, shift = back_terms(back_sums_ref[0:1], back_sums_ref[1:2], scale, root, root_offset, count)
    pre = dot(hidden_ref[...], w_c_ref[...])
    back = ((grad_ref[...].astype(full) * scale + pre * slope + shift) * inside).astype(low)
    back_ref[...] = back
    scale, offset, root, root_offset = norm_terms(sums_b_ref, params_b_ref, count)
    pre = pre_b_ref[...]
    grad = dot_cols(back, w_c_ref[...]) * inside * gelu_slope(pre * scale + offset)
    out_ref[...] = grad
    add_to(sums_ref, 0, total(grad))
    add_to(sums_ref, 1, total(grad * (pre * root + root_offset)))


def conv_b_back_kernel(edge_ref, count_ref, grad_ref, pre_b_ref, sums_b_ref, params_b_ref, back_sums_ref, pre_a_ref, sums_a_ref, params_a_ref, w_ref, back_ref, out_ref, sums_ref, wide_ref):
    count = count_ref[2:3, 0:1]
    inside = inside_of(edge_ref[0], CELLS)
    scale, _, root, root_offset = norm_terms(sums_b_ref, params_b_ref, count)
    slope, shift = back_terms(back_sums_ref[0:1], back_sums_ref[1:2], scale, root, root_offset, count)
    scale_a, offset_a, root_a, root_offset_a = norm_terms(sums_a_ref, params_a_ref, count)
    first = jnp.zeros((1, MID), full)
    second = first
    for one in range(grad_ref.shape[0] // CELLS):
        part = slice(one * CELLS, (one + 1) * CELLS)
        back = (grad_ref[part, :] * scale + pre_b_ref[part, :] * slope + shift) * inside
        back_ref[part, :] = back.astype(low)
        wide = wide_ref.at[one]
        spread_taps(back, wide)
        grad = jnp.zeros((CELLS, MID), full)
        for row_step in (-1, 0, 1):
            for col_step in (-1, 0, 1):
                tap = 3 * (row_step + 1) + col_step + 1
                at = GRID - GRID * row_step
                place = 1 - col_step
                grad += dot_cols(
                    wide[at : at + CELLS, place * MID : (place + 1) * MID], w_ref[tap]
                )
        pre = pre_a_ref[part, :]
        grad = grad * inside * gelu_slope(pre * scale_a + offset_a)
        out_ref[part, :] = grad
        first += total(grad)
        second += total(grad * (pre * root_a + root_offset_a))
    add_to(sums_ref, 0, first)
    add_to(sums_ref, 1, second)


def tap_grads_kernel(hidden_ref, back_ref, expand_ref, near_ref, far_ref, wide_ref, tall_ref):
    near = near_ref.shape[0]
    step = pl.program_id(0)

    @pl.when(step == 0)
    def _():
        rows = FRAMES * CELLS
        for frame in range(FRAMES):
            part = slice(frame * CELLS, (frame + 1) * CELLS)
            values = hidden_ref[part, :].astype(full)
            for col_step in (-1, 0, 1):
                moved = shift_columns(values, col_step).astype(low)
                wide_ref[col_step + 1, :, part] = moved.T
            back = back_ref[part, :]
            zero = jnp.zeros((GRID, MID), low)
            start = frame * CELLS
            tall_ref[0, start : start + CELLS - GRID, :] = back[GRID:]
            tall_ref[0, start + CELLS - GRID : start + CELLS, :] = zero
            tall_ref[1, part, :] = back
            tall_ref[2, start : start + GRID, :] = zero
            tall_ref[2, start + GRID : start + CELLS, :] = back[: CELLS - GRID]

    for tap in range(9):

        @pl.when(step == tap)
        def _():
            grads = dot(wide_ref[tap % 3], tall_ref[tap // 3]).astype(low)
            start = tap * MID - near
            if start < 0:
                near_ref[...] = grads[:near]
                far_ref[: MID - near, :] = grads[near:]
            else:
                far_ref[start : start + MID, :] = grads

    @pl.when(step == pl.num_programs(0) - 1)
    def _():
        far_ref[9 * MID - near :, :] = expand_ref[...]


def frame_grads_kernel(edge_ref, count_ref, grad_ref, pre_ref, sums_a_ref, params_ref, back_sums_ref, turned_ref, rest_ref, back_ref, out_ref):
    step = pl.program_id(0)
    rows = grad_ref.shape[0]

    @pl.when(step == 0)
    def _():
        count = count_ref[2:3, 0:1]
        inside = inside_of(edge_ref[0], CELLS)
        scale, _, root, root_offset = norm_terms(sums_a_ref, params_ref, count)
        slope, shift = back_terms(
            back_sums_ref[0:1], back_sums_ref[1:2], scale, root, root_offset, count
        )
        back_ref[:CELLS, :] = jnp.zeros((CELLS, MID), low)
        back_ref[rows + CELLS :, :] = jnp.zeros((CELLS, MID), low)
        for frame in range(FRAMES):
            part = slice(frame * CELLS, (frame + 1) * CELLS)
            back = (grad_ref[part, :] * scale + pre_ref[part, :] * slope + shift) * inside
            back_ref[(frame + 1) * CELLS : (frame + 2) * CELLS, :] = back.astype(low)

    blocks = turned_ref.shape[0] // MID
    offset = step // blocks
    across = pl.ds(pl.multiple_of((step - offset * blocks) * MID, MID), MID)
    start = pl.multiple_of((2 - offset) * CELLS, CELLS)
    place = pl.ds(pl.multiple_of(step * MID, MID), MID)
    out_ref[place, :] = dot(turned_ref[across, :], back_ref[pl.ds(start, rows), :]).astype(low)

    @pl.when(step == pl.num_programs(0) - 1)
    def _():
        out_ref[pl.num_programs(0) * MID :, :] = rest_ref[...]


def input_back_kernel(back_ref, grad_ref, w_ref, out_ref):
    step = pl.program_id(0)
    rows = grad_ref.shape[0]
    grad = grad_ref[...].astype(full)
    for offset in range(3):
        start = pl.multiple_of(step * rows + (2 - offset) * CELLS, CELLS)
        grad += dot_cols(back_ref[pl.ds(start, rows), :], w_ref[offset])
    out_ref[...] = grad.astype(low)


def on_device(
    clips_in,
    crop_edges,
    cotangent,
    bottle_weights,
    bottle_momentum,
    local_weights,
    local_momentum,
    norm_params,
    norm_momentum,
):
    clip_count, position_count, channels = clips_in.shape
    assert clip_count == 1 and position_count == FRAMES * CELLS
    rows = position_count
    keys = FRAMES * HALF
    x = clips_in.reshape(rows, channels)
    cot = cotangent.reshape(rows, channels)
    edge = (crop_edges, "smem")

    bits = bit_count()
    top = bits - 1
    inner = list(range(top - 1, -1, -1))
    mine = bottle_weights.astype(low).reshape(-1, MID)
    high, next_high = device_bit(top) == 1, device_bit(top - 1) == 1
    over = swap(mine, 1 << top)
    beyond = swap(mine, 1 << (top - 1))
    across = swap(mine, 3 << (top - 1))
    same = [jnp.where(next_high, beyond, mine), jnp.where(next_high, mine, beyond)]
    others = [jnp.where(next_high, across, over), jnp.where(next_high, over, across)]
    near = Gather(jnp.stack([jnp.where(high, b, a) for a, b in zip(same, others)]), inner)
    far = Gather(jnp.stack([jnp.where(high, a, b) for a, b in zip(same, others)]), inner)
    local_low = local_weights.astype(low).reshape(-1, INNER)
    turned = x.T
    for number in range(1, len(inner)):
        near.send()
        if number > 1:
            far.values = after(far.values, near.values)
            far.send()
        if 1 < number < len(inner) - 1:
            near.got = far.beside(near.got)
        if number == len(inner) - 2:
            near.got, turned, local_low = lax.optimization_barrier((near.got, turned, local_low))
        near.take()
        if 1 < number < len(inner) - 1:
            far.take()
    near_full = near.result()
    local_low = after(local_low, near_full)
    local_full = lax.all_gather(local_low, AXES, axis=0, tiled=True)
    first = 3 * channels
    weight_a = near_full[:first].reshape(3, channels, MID)
    w_in = local_full[: 3 * channels].reshape(3, channels, INNER)
    w_out = local_full[3 * channels :].reshape(INNER, channels)
    params_a = norm_params[: 2 * MID].reshape(2, MID)
    params_b = norm_params[2 * MID : 4 * MID].reshape(2, MID)
    params_c = norm_params[4 * MID : 4 * MID + 2 * channels].reshape(2, channels)
    params_n = norm_params[4 * MID + 2 * channels :].reshape(2, channels)

    step = STEP * CELLS
    steps = rows // step
    matmul = 2 * rows * MID * channels
    pre_a, part = call(
        conv_a_kernel,
        steps,
        [edge, (x, step), (weight_a, None)],
        [(shape((rows, MID), full), None), (shape((3, MID), full), None)],
        flops=3 * matmul,
        name="conv_a",
    )
    part = far.beside(part)
    far.take()
    far.send()
    sums_a = far.beside(sum_small(part) if WHOLE & 1 else sum_devices(part))
    far.take()
    far_full = far.result()
    rest = first + 9 * MID - near_full.shape[0]
    weight_b = jnp.concatenate([near_full[first:], far_full[:rest]])
    weight_c = far_full[rest:].reshape(MID, channels)
    count = (sums_a, None)
    hidden_a, pre_b, part = call(
        conv_b_kernel,
        steps,
        [edge, count, (pre_a, step), (sums_a, None), (params_a, None), (weight_b.reshape(3, 3 * MID, MID), None)],
        [(kept((rows, MID), low), step), (shape((rows, MID), full), step), (shape((2, MID), full), None)],
        [pltpu.VMEM((step // CELLS, CELLS + 2 * GRID, 3 * MID), low)],
        flops=9 * matmul // 4,
        name="conv_b",
    )
    sums_b = sum_small(part) if WHOLE & 1 else sum_devices(part)
    hidden_b, part = call(
        conv_c_kernel,
        steps,
        [edge, count, (pre_b, step), (sums_b, None), (params_b, None), (weight_c, None)],
        [(shape((rows, MID), low), step), (shape((2, channels), full), None)],
        flops=matmul,
        name="conv_c",
    )
    sums_c = sum_pairs(part) if PAIRS & 1 else sum_devices(part)
    mixed, pooled, query, key_rows, value_rows = call(
        embed_kernel,
        steps,
        [edge, count, (hidden_b, step), (x, step), (sums_c, None), (params_c, None), (weight_c, None), (w_in, None)],
        [
            (kept((rows, channels), low), step),
            (kept((keys, channels), low), step // 4),
            (shape((rows, INNER), low), step),
            (shape((keys, INNER), low), step // 4),
            (shape((keys, INNER), low), step // 4),
        ],
        flops=4 * matmul,
        name="embed",
    )
    probs, attended, pre_w, part = call(
        attend_kernel,
        steps,
        [edge, (query, step), (key_rows, None), (value_rows, None), (w_out, None), (cot, step)],
        [
            (kept((rows, keys), low), step),
            (kept((rows, INNER), low), step),
            (kept((rows, channels), low), step),
            (shape((4, channels), full), None),
        ],
        flops=4 * matmul,
        name="attend",
    )
    sums_n = sum_devices(part)
    clips_out, back_w, grad_query, grad_key, grad_value, grad_pooled = call(
        attend_back_kernel,
        steps,
        [
            edge,
            count,
            (pre_w, step),
            (mixed, step),
            (cot, step),
            (probs, step),
            (query, step),
            (key_rows, None),
            (value_rows, None),
            (w_out, None),
            (w_in, None),
            (sums_n, None),
            (params_n, None),
        ],
        [
            (shape((rows, channels), low), step),
            (shape((rows, channels), low), step),
            (shape((rows, INNER), low), step),
            (shape((keys, INNER), low), None),
            (shape((keys, INNER), low), None),
            (shape((2 * keys, channels), low), None),
        ],
        [pltpu.VMEM((keys, INNER), full), pltpu.VMEM((keys, INNER), full)],
        flops=7 * matmul,
        name="attend_back",
    )
    shard_rows = local_low.shape[0]
    pairs = device_count() // 2
    if shard_rows % 32 == 0:

        def columns(width, at):
            return pl.BlockSpec((rows, width), lambda i: (0, at(i)))

        (local_grads,) = call(
            local_grads_kernel,
            8,
            [
                (mixed, columns(2 * MID, lambda i: jnp.minimum(i, 1))),
                (grad_query, None),
                (pooled, pl.BlockSpec((keys, 2 * MID), lambda i: (0, i & 1))),
                (grad_key, None),
                (grad_value, None),
                (attended, columns(MID, lambda i: jnp.maximum(i - 6, 0))),
                (back_w, None),
            ],
            [
                (
                    shape((2, pairs, shard_rows, INNER), low),
                    pl.BlockSpec((2, pairs // 8, shard_rows, INNER), lambda i: (0, i, 0, 0)),
                )
            ],
            flops=5 * matmul,
            name="local_grads",
        )
    else:
        grad_out = dot_rows(attended, back_w).astype(low)
        grad_out = grad_out.reshape(-1, shard_rows // 2, 2, INNER).transpose(0, 2, 1, 3)
        local_grads = jnp.concatenate(
            [
                dot_rows(mixed, grad_query).astype(low),
                dot_rows(pooled, grad_key).astype(low),
                dot_rows(pooled, grad_value).astype(low),
                grad_out.reshape(-1, INNER),
            ]
        )
        local_grads = local_grads.reshape(pairs, 2, shard_rows, INNER).transpose(1, 0, 2, 3)
    spans = list(range(top, 0, -1))
    local = Scatter(local_grads, [0], [0] + spans)
    local.send()
    grad_query = local.beside(grad_query)
    local.take()
    local = Halves(local.values, 1, top, spans)
    local.send()
    grad_joined, part = call(
        joined_back_kernel,
        steps,
        [
            edge,
            count,
            (hidden_b, step),
            (x, step),
            (cot, step),
            (grad_query, step),
            (grad_pooled, step // 2),
            (weight_c, None),
            (w_in, None),
            (sums_c, None),
            (params_c, None),
        ],
        [(shape((rows, channels), low), step), (shape((2, channels), full), None)],
        flops=4 * matmul,
        name="joined_back",
    )
    part = local.beside(part)
    local.take()
    local.send()
    back_sums_c = local.beside(sum_pairs(part) if PAIRS & 2 else sum_devices(part))
    local.take()
    local = local.whole(range(2, top))
    local.send()
    back_c, grad_b, part = call(
        expand_back_kernel,
        steps,
        [
            edge,
            count,
            (grad_joined, step),
            (hidden_b, step),
            (pre_b, step),
            (weight_c, None),
            (sums_c, None),
            (params_c, None),
            (back_sums_c, None),
            (sums_b, None),
            (params_b, None),
        ],
        [
            (shape((rows, channels), low), step),
            (shape((rows, MID), full), step),
            (shape((2, MID), full), None),
        ],
        flops=2 * matmul,
        name="expand_back",
    )
    back_sums_b = local.beside(sum_small(part) if WHOLE & 2 else sum_devices(part))
    local.take()
    local.send()
    grad_weight_c = dot_rows(hidden_b, back_c).astype(low)
    back_b, grad_a, part = call(
        conv_b_back_kernel,
        steps,
        [
            edge,
            count,
            (grad_b, step),
            (pre_b, step),
            (sums_b, None),
            (params_b, None),
            (back_sums_b, None),
            (pre_a, step),
            (sums_a, None),
            (params_a, None),
            (weight_b.reshape(9, MID, MID), None),
        ],
        [
            (shape((rows, MID), low), step),
            (shape((rows, MID), full), step),
            (shape((2, MID), full), None),
        ],
        [pltpu.VMEM((step // CELLS, CELLS + 2 * GRID, 3 * MID), low)],
        flops=9 * matmul // 4,
        name="conv_b_back",
    )
    half = near_full.shape[0]
    near_grads, far_grads = call(
        tap_grads_kernel,
        10,
        [(hidden_a, None), (back_b, None), (grad_weight_c.reshape(-1, MID), None)],
        [(shape((half - first, MID), low), None), (shape((half, MID), low), None)],
        [pltpu.VMEM((3, MID, rows), low), pltpu.VMEM((3, rows, MID), low)],
        flops=9 * matmul // 4,
        name="tap_grads",
    )
    part = local.beside(part)
    local.take()
    while local.order:
        local.send()
        local.take()
    spans = list(range(top - 1, 0, -1))
    far = Scatter(far_grads, [0], spans + [0])
    far.send()
    if WHOLE & 2:
        back_sums_a = far.beside(sum_small(part))
    else:
        back_sums_a = sum_devices(part, far.beside)
    far.take()
    far = Halves(far.values, 1, 2, spans)
    far.send()
    padded, near_grads = call(
        frame_grads_kernel,
        first // MID,
        [
            edge,
            count,
            (grad_a, None),
            (pre_a, None),
            (sums_a, None),
            (params_a, None),
            (back_sums_a, None),
            (turned, None),
            (near_grads, None),
        ],
        [(shape((rows + 2 * CELLS, MID), low), None), (shape((half, MID), low), None)],
        flops=3 * matmul,
        name="frame_grads",
    )
    near_grads = far.beside(near_grads)
    near = Scatter(near_grads, [0], spans + [0])
    near.send()
    far.take()
    far.send()
    padded = near.beside(padded)
    near.take()
    near = Halves(near.values, 1, 2, spans)
    near.send()
    (clips_grad,) = call(
        input_back_kernel,
        steps,
        [(padded, None), (grad_joined, step), (weight_a, None)],
        [(shape((rows, channels), low), step)],
        flops=3 * matmul,
        name="input_back",
    )
    clips_grad = near.beside(far.beside(clips_grad))
    near.take()
    near.send()
    far.take()
    far = far.whole(range(3, top - 1))
    while far.order:
        far.send()
        far.take()
    near.take()
    near = near.whole(range(3, top - 1))
    while near.order:
        near.send()
        near.take()
    same = [jnp.where(high, b, a) for a, b in zip(near.values, far.values)]
    others = [jnp.where(high, a, b) for a, b in zip(near.values, far.values)]
    over = swap(jnp.where(next_high, others[1], others[0]), 1 << top)
    beyond = swap(jnp.where(next_high, same[0], same[1]), 1 << (top - 1))
    across = swap(jnp.where(next_high, others[0], others[1]), 3 << (top - 1))
    own = jnp.where(next_high, same[1], same[0])
    bottle_shard = (
        (own.astype(full) + over.astype(full)) + (beyond.astype(full) + across.astype(full))
    ).reshape(-1)
    local_sum = local.values.astype(full)
    halves = local_sum.reshape(2, -1, INNER)
    joint = jnp.concatenate([halves[0], halves[1]], axis=1).reshape(-1)
    in_out = lax.axis_index(AXES) * shard_rows >= 3 * channels
    local_shard = jnp.where(in_out, joint, local_sum.reshape(-1))
    clips_total = clip_count * device_count()
    mean_n, root_n = moments(sums_n, sums_a[2, 0])
    gain_n_grad = root_n[0] * (sums_n[3] - mean_n[0] * sums_n[2])
    norm_grad = jnp.concatenate(
        [
            back_sums_a[1],
            back_sums_a[0],
            back_sums_b[1],
            back_sums_b[0],
            back_sums_c[1],
            back_sums_c[0],
            gain_n_grad,
            sums_n[2],
        ]
    )
    bottle_velocity = (
        momentum_rate * bottle_momentum + bottle_shard / clips_total + decay_rate * bottle_weights
    )
    local_velocity = (
        momentum_rate * local_momentum + local_shard / clips_total + decay_rate * local_weights
    )
    norm_velocity = momentum_rate * norm_momentum + norm_grad / clips_total
    return (
        clips_out.reshape(clips_in.shape),
        clips_grad.reshape(clips_in.shape),
        bottle_weights - learning_rate * bottle_velocity,
        bottle_velocity,
        local_weights - learning_rate * local_velocity,
        local_velocity,
        norm_params - learning_rate * norm_velocity,
        norm_velocity,
    )


def solution(mesh):
    devices = mesh.devices.reshape(mesh.shape["dp"], mesh.shape["fsdp"] // 2, 2)
    split = P(AXES)
    return jax.shard_map(
        on_device,
        mesh=Mesh(devices, AXES),
        in_specs=(split,) * 7 + (P(),) * 2,
        out_specs=(split,) * 6 + (P(),) * 2,
        check_vma=False,
    )
```
